128 devices in a mesh: dp: 4 (over x), expert: 32 (over z, y, core).
Axes of the slice: x: 4, y: 4, z: 4, core: 2. Of those that a mesh axis runs over, the one named last changes fastest.
Arguments:
- tokens: bfloat16 [16384, 2048], P(('dp', 'expert')), may hold values from -6 to 6
- expert_ids: int32 [16384, 4], P(('dp', 'expert')), may hold values from 0 to 63, all different within a row; in each aligned block of 128 rows (0 to 127, 128 to 255, ...) at most 14 rows name the same one
- gate_weights: float32 [16384, 4], P(('dp', 'expert')), may hold values from 0.05 to 0.5
- slot_of_expert: int32 [64], replicated, may hold values from 0 to 63, each once
- w_gate: bfloat16 [64, 2048, 768], P('expert'), may hold values from -0.125 to 0.125
- w_up: bfloat16 [64, 2048, 768], P('expert'), may hold values from -0.125 to 0.125
- w_down: bfloat16 [64, 768, 2048], P('expert'), may hold values from -0.21875 to 0.21875
- d_out: bfloat16 [16384, 2048], P(('dp', 'expert')), may hold values from -6 to 6
Outputs:
- layer_out: bfloat16 [16384, 2048], P(('dp', 'expert'))
- d_tokens: bfloat16 [16384, 2048], P(('dp', 'expert'))
- d_gates: float32 [16384, 4], P(('dp', 'expert'))
- grad_gate: bfloat16 [64, 2048, 768], P('expert', 'dp')
- grad_up: bfloat16 [64, 2048, 768], P('expert', 'dp')
- grad_down: bfloat16 [64, 768, 2048], P('expert', None, 'dp')
The draws below stay inside these ranges and needn't reach their ends.
Inputs may be any that keep to these rules, and one draw needn't show every extreme that they name: `expert_ids`: each row names 4 different experts. Among the 128 rows of one device (aligned blocks of rows) no expert is named more than 14 times, and in every draw some expert is named exactly 14 times in some block. A permutation: expert e's weights stand at index slot_of_expert[e] of w_gate, w_up and w_down, and its gradients at that index of the outputs.
All inputs are finite; a program needn't handle non-finite values.
Results may differ from the reference program's by a relative error of at most 0.0095.
Values may be sent and summed in bfloat16 or wider, within the bound.
A program may use at most 192 MiB of HBM per device.

```python
import math
import jax
import jax.numpy as jnp
import numpy as np
from jax import lax

D = 2048
FF = 768
TOP = 4
TOK_DEV = 128
EXPERTS = 64
CAP = 14
TOKENS = 16384
N_DP = 4
N_EXPERT = 32


def block_scale(stream_key, shape, cuts, smallest, top_value):
    factor_of = 1.0
    for position, parts in cuts:
        draws = jax.random.uniform(jax.random.fold_in(jax.random.fold_in(stream_key, 6), position), (parts,), jnp.float32, smallest / len(cuts), top_value / len(cuts))
        factor_of = factor_of * jnp.repeat(jnp.exp(draws), shape[position] // parts).reshape((-1,) + (1,) * (len(shape) - 1 - position))
    return factor_of


def assign_block(rng, own, number, rows, amount, top, bound, lean):
    sequence = jax.random.permutation(rng, amount)
    packed, ordinary = load_shares(amount, rows * top, bound, lean, True), load_shares(amount, rows * top, bound, lean, False)
    places = jnp.arange(amount)

    def named(tallies, turn):
        used = int((tallies > 0).sum())
        fixed = max(1, used // 4)
        passed = fixed + (places - fixed + turn * (used - fixed)) % max(1, amount - fixed)
        return jnp.zeros((amount,), jnp.int32).at[sequence[jnp.where(places < fixed, places, passed)]].set(jnp.asarray(tallies, jnp.int32))

    tallies = jnp.where(number % 4 == 0, named(packed, number // 4), named(ordinary, number - number // 4 - 1))
    mixed = jax.random.permutation(jax.random.fold_in(own, 3), amount)
    donor, sink = mixed[0:amount // 2 * 2:2], mixed[1:amount // 2 * 2:2]
    margin = jnp.minimum(tallies[donor] - 1, bound - tallies[sink]) // 2
    margin = jnp.where((donor == sequence[0]) | (sink == sequence[0]) | (tallies[sink] == 0), 0, jnp.maximum(margin, 0))
    passed = jax.random.randint(jax.random.fold_in(own, 4), (amount // 2,), 0, 1 << 20) % (margin + 1)
    tallies = tallies.at[donor].add(-passed).at[sink].add(passed)
    labels = jnp.searchsorted(jnp.cumsum(tallies), jnp.arange(rows * top), side="right").astype(jnp.int32)
    grid = labels.reshape(top, rows).T
    grid = grid[jax.random.permutation(jax.random.fold_in(own, 1), rows)]
    turn = jax.random.randint(jax.random.fold_in(own, 2), (rows, 1), 0, top)
    return jnp.take_along_axis(grid, (jnp.arange(top)[None, :] + turn) % top, axis=1)


def load_shares(count, total, reach, lean, full):
    portions = [(1 << 20) // math.isqrt(rank ** lean) + 1 for rank in range(1, count + 1)]
    largest = reach if full else min(reach, max(-(-total // count), total * portions[0] // sum(portions)))
    least = 1 if total - largest >= count - 1 else 0
    given, spare = [largest] + [least] * (count - 1), total - largest - least * (count - 1)
    while spare > 0:
        free = [i for i in range(1, count) if given[i] < largest] or [i for i in range(1, count) if given[i] < reach]
        whole, left = sum([portions[i] for i in free]), spare
        for i in free:
            extra = min(reach - given[i], max(1, left * portions[i] // whole), spare)
            given[i] = given[i] + extra
            spare = spare - extra
    return np.array(given)


def scatter_about(key, shape, width, bound, shards=(), held_as=jnp.bfloat16):
    level = block_scale(key, shape, shards, -0.22, 0.18) if shards else 1.0
    entries = jax.random.normal(key, shape, jnp.float32) * width * level
    return jnp.minimum(jnp.maximum(entries, -bound), bound).astype(held_as)


def setup_inputs(seed: int = 0) -> dict:
    keys = jax.random.split(jax.random.key(seed), 9)
    tokens = scatter_about(keys[0], (TOKENS, D), 1.0, 6.0, ((0, 128),))
    expert_ids_keys = jax.random.split(jax.random.fold_in(keys[1], 1), TOKENS // TOK_DEV)
    expert_ids_turns = jax.random.permutation(jax.random.fold_in(keys[1], 3), TOKENS // TOK_DEV)
    expert_ids = jax.vmap(lambda own, number: assign_block(jax.random.fold_in(keys[1], 2), own, number, TOK_DEV, EXPERTS, TOP, CAP, 2))(expert_ids_keys, expert_ids_turns).reshape((TOKENS, TOP))
    gate_weights = jnp.clip(0.05 + 0.45 * jax.random.uniform(keys[2], (TOKENS, TOP), jnp.float32) ** block_scale(keys[2], (TOKENS, TOP), ((0, 128),), -0.2, 0.2), 0.05, 0.5)
    slot_of_expert = jax.random.permutation(keys[3], EXPERTS).astype(jnp.int32)
    w_gate = scatter_about(keys[4], (EXPERTS, D, FF), D ** -0.5, 0.125, ((0, 32),))
    w_up = scatter_about(keys[5], (EXPERTS, D, FF), D ** -0.5, 0.125, ((0, 32),))
    w_down = scatter_about(keys[6], (EXPERTS, FF, D), FF ** -0.5, 0.21875, ((0, 32),))
    d_out = scatter_about(keys[7], (TOKENS, D), 1.0, 6.0, ((0, 128),))
    return dict(tokens=tokens, expert_ids=expert_ids, gate_weights=gate_weights, slot_of_expert=slot_of_expert, w_gate=w_gate, w_up=w_up, w_down=w_down, d_out=d_out)


def take_rows(source_rows, row_ids):
    return source_rows[row_ids]


def reference(tokens, expert_ids, gate_weights, slot_of_expert, w_gate, w_up, w_down, d_out):
    per_group = TOK_DEV * N_EXPERT
    count = per_group * TOP
    most_rows = CAP * N_EXPERT
    slots = slot_of_expert[expert_ids].astype(jnp.int32).reshape(N_DP, count)
    expert_range = jnp.arange(EXPERTS, dtype=jnp.int32)
    onehot = (slots[:, :, None] == expert_range).astype(jnp.int32)
    ranks = jnp.sum((jnp.cumsum(onehot, axis=1) - 1) * onehot, axis=2).astype(jnp.int32)
    group_rows = jnp.broadcast_to(jnp.arange(N_DP, dtype=jnp.int32)[:, None], (N_DP, count))
    assign_ids = jnp.broadcast_to(jnp.arange(count, dtype=jnp.int32)[None, :], (N_DP, count))
    table_ids = jnp.full((N_DP, EXPERTS, most_rows), count, jnp.int32)
    table_ids = table_ids.at[group_rows, slots, ranks].set(assign_ids)
    zero_row = jnp.zeros((N_DP, 1, D), jnp.bfloat16)
    tok_padded = jnp.concatenate([tokens.reshape(N_DP, per_group, D), zero_row], axis=1)
    d_routed = (gate_weights[:, :, None] * d_out[:, None, :].astype(jnp.float32)).astype(jnp.bfloat16)
    dy_padded = jnp.concatenate([d_routed.reshape(N_DP, count, D), zero_row], axis=1)

    def per_slot(slot_index):
        assign = lax.dynamic_index_in_dim(table_ids, slot_index, 1, keepdims=False)
        owners = (assign // TOP).astype(jnp.int32)
        inputs = jax.vmap(take_rows)(tok_padded, owners).astype(jnp.float32)
        d_rows = jax.vmap(take_rows)(dy_padded, assign).astype(jnp.float32)
        gate_mat = lax.dynamic_index_in_dim(w_gate, slot_index, 0, keepdims=False).astype(jnp.float32)
        up_mat = lax.dynamic_index_in_dim(w_up, slot_index, 0, keepdims=False).astype(jnp.float32)
        down_mat = lax.dynamic_index_in_dim(w_down, slot_index, 0, keepdims=False).astype(jnp.float32)
        pre_gate = jnp.einsum("rcd,df->rcf", inputs, gate_mat)
        pre_up = jnp.einsum("rcd,df->rcf", inputs, up_mat)
        sigma = jax.nn.sigmoid(pre_gate)
        silu_gate = pre_gate * sigma
        hidden = (silu_gate * pre_up).astype(jnp.bfloat16)
        outputs = jnp.einsum("rcf,fd->rcd", hidden.astype(jnp.float32), down_mat).astype(jnp.bfloat16)
        d_hidden = jnp.einsum("rcd,fd->rcf", d_rows, down_mat)
        d_gate_pre = (d_hidden * pre_up * sigma * (1.0 + pre_gate * (1.0 - sigma))).astype(jnp.bfloat16)
        d_up_pre = (d_hidden * silu_gate).astype(jnp.bfloat16)
        d_inputs = jnp.einsum("rcf,df->rcd", d_gate_pre.astype(jnp.float32), gate_mat)
        d_inputs = d_inputs + jnp.einsum("rcf,df->rcd", d_up_pre.astype(jnp.float32), up_mat)
        d_inputs = d_inputs.astype(jnp.bfloat16)
        part_gate = jnp.einsum("rcd,rcf->rdf", inputs, d_gate_pre.astype(jnp.float32))
        part_up = jnp.einsum("rcd,rcf->rdf", inputs, d_up_pre.astype(jnp.float32))
        part_down = jnp.einsum("rcf,rcd->rfd", hidden.astype(jnp.float32), d_rows)
        part_gate = lax.optimization_barrier(part_gate.astype(jnp.bfloat16)).astype(jnp.float32)
        part_up = lax.optimization_barrier(part_up.astype(jnp.bfloat16)).astype(jnp.float32)
        part_down = lax.optimization_barrier(part_down.astype(jnp.bfloat16)).astype(jnp.float32)
        return (outputs, d_inputs, jnp.sum(part_gate, axis=0).astype(jnp.bfloat16),
                jnp.sum(part_up, axis=0).astype(jnp.bfloat16), jnp.sum(part_down, axis=0).astype(jnp.bfloat16))

    outs_all, d_in_all, grad_gate, grad_up, grad_down = lax.map(per_slot, expert_range)
    expert_out = outs_all[slots, group_rows, ranks].reshape(N_DP * per_group, TOP, D).astype(jnp.float32)
    d_routed_in = d_in_all[slots, group_rows, ranks].reshape(N_DP * per_group, TOP, D).astype(jnp.float32)
    layer_out = jnp.sum(gate_weights[:, :, None] * expert_out, axis=1).astype(jnp.bfloat16)
    d_gates = jnp.sum(d_out[:, None, :].astype(jnp.float32) * expert_out, axis=2)
    d_tokens = jnp.sum(d_routed_in, axis=1).astype(jnp.bfloat16)
    return (layer_out, d_tokens, d_gates, grad_gate, grad_up, grad_down)
```

```python
import functools

import jax
import jax.numpy as jnp
from jax import lax
from jax.experimental import pallas as pl
from jax.experimental.pallas import tpu as pltpu
from jax.sharding import PartitionSpec as P

MESH = pl.DeviceIdType.MESH
F32 = jnp.float32
BF16 = jnp.bfloat16
NT = (((1,), (1,)), ((), ()))
TN = (((0,), (0,)), ((), ()))


def mm(a, b):
    return jnp.dot(a, b, preferred_element_type=F32)


def mm_nt(a, b):
    return lax.dot_general(a, b, NT, preferred_element_type=F32)


def mm_tn(a, b):
    return lax.dot_general(a, b, TN, preferred_element_type=F32)


def kernel(
    n, ring, pos_t, pos, gates_t, gates, tok, dout, wg_h, wu_h, wd_h,
    lo, dt, dg, gg, gu, gd, ret, r2w, r2d,
    send, land, wg, wu, wd, act, hid, pw, pd, r1w, r1d, tw, td,
    f_send, f_recv, b_send, b_recv, w_sem, g_send, g_recv, l_sem, o_sem,
):
    me = lax.axis_index("expert")
    r = lax.axis_index("dp")
    right, left, opp = lax.rem(r + 1, ring), lax.rem(r + 3, ring), lax.rem(r + 2, ring)
    slots, _, pad, width = send.shape[1:]
    rows = n * pad
    ff = wg.shape[1]
    chunk = width // ring
    ft = 256
    tops = gates.shape[1]

    barrier = pltpu.get_barrier_semaphore()

    def greet(i, _):
        pl.semaphore_signal(
            barrier, inc=1, device_id={"expert": lax.rem(me + i, n)}, device_id_type=MESH
        )
        return 0

    lax.fori_loop(1, n, greet, 0)
    for side in (right, left):
        pl.semaphore_signal(barrier, inc=1, device_id={"dp": side}, device_id_type=MESH)

    def weight_copies(s):
        return [
            pltpu.make_async_copy(src.at[s], dst, w_sem.at[j])
            for j, (src, dst) in enumerate(((wg_h, wg), (wu_h, wu), (wd_h, wd)))
        ]

    for copy in weight_copies(0):
        copy.start()

    def fill(s):
        spot = lax.broadcasted_iota(jnp.int32, (rows, pos_t.shape[1]), 0) + s * rows
        picked = jnp.zeros(spot.shape, F32)
        weight = jnp.zeros(spot.shape, F32)
        for k in range(tops):
            hit = pos_t[k : k + 1, :] == spot
            picked = jnp.where(hit, 1.0, picked)
            weight = jnp.where(hit, gates_t[k : k + 1, :], weight)
        picked = picked.astype(BF16)
        weight = jnp.sum(weight, axis=1, keepdims=True)

        def tile(j, _):
            cols = pl.ds(pl.multiple_of(j * chunk, chunk), chunk)
            send[0, s, :, :, cols] = mm(picked, tok[:, cols]).astype(BF16).reshape(n, pad, chunk)
            rows_d = mm(picked, dout[:, cols]) * weight
            send[1, s, :, :, cols] = rows_d.astype(BF16).reshape(n, pad, chunk)
            return 0

        lax.fori_loop(0, width // chunk, tile, 0)

    def exchange(k, s, dst, s_sem, r_sem):
        pltpu.make_async_copy(send.at[k, s, me], dst.at[k, s, me], r_sem.at[k, s]).start()

        def go(i, _):
            peer = lax.rem(me + i, n)
            pltpu.make_async_remote_copy(
                src_ref=send.at[k, s, peer],
                dst_ref=dst.at[k, s, me],
                send_sem=s_sem.at[k, s],
                recv_sem=r_sem.at[k, s],
                device_id={"expert": peer},
                device_id_type=MESH,
            ).start()
            return 0

        lax.fori_loop(1, n, go, 0)

    def wait_recv(k, s, dst, r_sem):
        pltpu.make_async_copy(dst.at[k, s], dst.at[k, s], r_sem.at[k, s]).wait()

    def wait_send(k, s, s_sem):
        part = send.at[k, s, pl.ds(0, n - 1)]
        pltpu.make_async_copy(part, part, s_sem.at[k, s]).wait()

    items = (
        (pd, r1d, r2d, td, gd),
        (pw.at[0], r1w.at[0], r2w.at[0], tw, gg),
        (pw.at[1], r1w.at[1], r2w.at[1], tw, gu),
    )

    def ring_copy(item, s, step, side):
        part, first, second, _, _ = items[item]
        half = part.shape[2] // 2
        low, high = pl.ds(0, half), pl.ds(half, half)
        near = right if side == 0 else left
        if step == 0:
            rows_s = low if side == 0 else high
            src, dst = part.at[s, opp, rows_s], first.at[s, side]
        else:
            rows_s = (high if side == 0 else low) if step == 1 else (low if side == 0 else high)
            src, dst = part.at[s, near, rows_s], second.at[s, side, rows_s]
        return pltpu.make_async_remote_copy(
            src_ref=src,
            dst_ref=dst,
            send_sem=g_send.at[s, item, step, side],
            recv_sem=g_recv.at[s, item, step, side],
            device_id={"dp": near},
            device_id_type=MESH,
        )

    def ring_start(item, s):
        for step in (0, 1):
            for side in (0, 1):
                ring_copy(item, s, step, side).start()

    def add_rows(dst, src, count):
        block = 64

        def go(j, _):
            at = pl.ds(pl.multiple_of(j * block, block), block)
            dst[at, :] = (dst[at, :].astype(F32) + src[at, :].astype(F32)).astype(BF16)
            return 0

        lax.fori_loop(0, count // block, go, 0)

    def ring_middle(item, s):
        part, first, _, _, _ = items[item]
        half = part.shape[2] // 2
        for side in (0, 1):
            near = right if side == 0 else left
            at = pl.ds(0, half) if side == 0 else pl.ds(half, half)
            ring_copy(item, s, 0, side).wait_recv()
            add_rows(part.at[s, near, at], first.at[s, side], half)
            ring_copy(item, s, 2, side).start()

    def ring_end(item, s):
        part, _, second, temp, out = items[item]
        count = part.shape[2]
        for side in (0, 1):
            for step in (1, 2):
                ring_copy(item, s, step, side).wait_recv()
        loads = [
            pltpu.make_async_copy(second.at[s, side], temp.at[side], l_sem.at[side])
            for side in (0, 1)
        ]
        for copy in loads:
            copy.start()
        for copy in loads:
            copy.wait()
        block = 64
        own = part.at[s, r]

        def go(j, _):
            at = pl.ds(pl.multiple_of(j * block, block), block)
            total = own[at, :].astype(F32) + temp[0, at, :].astype(F32) + temp[1, at, :].astype(F32)
            own[at, :] = total.astype(BF16)
            return 0

        lax.fori_loop(0, count // block, go, 0)
        pltpu.make_async_copy(own, out.at[s], o_sem.at[s, item]).start()

    def rows_of(k, s, cols):
        return land[k, s, :, :, cols].reshape(rows, -1)

    def compute(s, _):
        for copy in weight_copies(s):
            copy.wait()
        wait_recv(0, s, land, f_recv)

        def first(j, _):
            cols = pl.ds(pl.multiple_of(j * ft, ft), ft)
            x = rows_of(0, s, slice(None))
            gate = mm(x, wg[:, cols])
            up = mm(x, wu[:, cols])
            sigma = jax.nn.sigmoid(gate)
            silu = gate * sigma
            hid[0, :, cols] = (silu * up).astype(BF16)
            act[0, :, cols] = up * sigma * (1.0 + gate * (1.0 - sigma))
            act[1, :, cols] = silu
            return 0

        lax.fori_loop(0, ff // ft, first, 0)
        wait_send(0, s, f_send)

        def out_tile(j, _):
            cols = pl.ds(pl.multiple_of(j * chunk, chunk), chunk)
            send[0, s, :, :, cols] = mm(hid[0], wd[:, cols]).astype(BF16).reshape(n, pad, chunk)
            return 0

        lax.fori_loop(0, ring, out_tile, 0)
        exchange(0, s, ret, b_send, b_recv)

        wait_recv(1, s, land, f_recv)

        def down_tile(j, _):
            cols = pl.ds(pl.multiple_of(j * chunk, chunk), chunk)
            pd[s, j] = mm_tn(hid[0], rows_of(1, s, cols)).astype(BF16)
            return 0

        lax.fori_loop(0, ring, down_tile, 0)
        ring_start(0, s)

        def back(j, _):
            cols = pl.ds(pl.multiple_of(j * ft, ft), ft)
            d_hid = mm_nt(rows_of(1, s, slice(None)), wd[cols, :])
            hid[1, :, cols] = (d_hid * act[0, :, cols]).astype(BF16)
            hid[2, :, cols] = (d_hid * act[1, :, cols]).astype(BF16)
            return 0

        lax.fori_loop(0, ff // ft, back, 0)
        for item in (0, 1):

            def up_tile(j, _):
                cols = pl.ds(pl.multiple_of(j * chunk, chunk), chunk)
                pw[item, s, j] = mm_tn(rows_of(0, s, cols), hid[1 + item]).astype(BF16)
                return 0

            lax.fori_loop(0, ring, up_tile, 0)
            ring_start(1 + item, s)
        wait_send(1, s, f_send)

        def in_tile(j, _):
            cols = pl.ds(pl.multiple_of(j * chunk, chunk), chunk)
            total = mm_nt(hid[1], wg[cols, :]) + mm_nt(hid[2], wu[cols, :])
            send[1, s, :, :, cols] = total.astype(BF16).reshape(n, pad, chunk)
            return 0

        lax.fori_loop(0, ring, in_tile, 0)
        exchange(1, s, ret, b_send, b_recv)

        @pl.when(s + 1 < slots)
        def _():
            for copy in weight_copies(s + 1):
                copy.start()

        for item in range(3):
            ring_middle(item, s)
        return 0

    fill(0)
    pl.semaphore_wait(barrier, n + 1)
    for k in (0, 1):
        exchange(k, 0, land, f_send, f_recv)
    for s in range(1, slots):
        fill(s)
        for k in (0, 1):
            exchange(k, s, land, f_send, f_recv)
    lax.fori_loop(0, slots, compute, 0)

    spots = slots * rows
    loads = [pltpu.make_async_copy(ret.at[k], land.at[k], l_sem.at[k]) for k in (0, 1)]
    for k in (0, 1):
        for s in range(slots):
            wait_recv(k, s, ret, b_recv)
        loads[k].start()
    spot = lax.broadcasted_iota(jnp.int32, (pos.shape[0], spots), 1)
    hits = [pos[:, k : k + 1] == spot for k in range(tops)]
    hits = [jnp.where(hit, 1.0, 0.0) for hit in hits]
    whole = sum(hits).astype(BF16)
    hits = [hit.astype(BF16) for hit in hits]
    for copy in loads:
        copy.wait()

    def combine(j, sums):
        cols = pl.ds(pl.multiple_of(j * chunk, chunk), chunk)
        outs = land[0, :, :, :, cols].reshape(spots, chunk)
        d_ins = land[1, :, :, :, cols].reshape(spots, chunk)
        d_here = dout[:, cols].astype(F32)
        layer = jnp.zeros(d_here.shape, F32)
        result = []
        for k in range(tops):
            got = mm(hits[k], outs)
            layer = layer + gates[:, k : k + 1] * got
            result.append(sums[k] + jnp.sum(d_here * got, axis=1, keepdims=True))
        lo[:, cols] = layer.astype(BF16)
        dt[:, cols] = mm(whole, d_ins).astype(BF16)
        return tuple(result)

    zero = jnp.zeros((pos.shape[0], 1), F32)
    sums = lax.fori_loop(0, ring, combine, (zero,) * tops)
    for k in range(tops):
        dg[:, k : k + 1] = sums[k]

    for s in range(slots):
        for item in range(3):
            ring_end(item, s)
    for s in range(slots):
        for item in range(3):
            part, _, _, _, out = items[item]
            pltpu.make_async_copy(part.at[s, r], out.at[s], o_sem.at[s, item]).wait()
            for step in range(3):
                for side in (0, 1):
                    ring_copy(item, s, step, side).wait_send()
        for k in (0, 1):
            wait_send(k, s, b_send)


def on_device(n, ring, tokens, expert_ids, gate_weights, slot_of_expert, w_gate, w_up, w_down, d_out):
    slots, width, ff = w_gate.shape
    tok_rows, tops = expert_ids.shape
    experts = slots * n
    capacity = tok_rows * tops * 7 // (4 * experts)
    pad = -(-capacity // 16) * 16
    rows = n * pad
    chunk = width // ring

    wide = jnp.arange(experts, dtype=jnp.int32)
    slot = jnp.sum(jnp.where(expert_ids[:, :, None] == wide, slot_of_expert, 0), axis=2)
    named = slot[:, :, None] == wide
    earlier = jnp.arange(tok_rows)[:, None] > jnp.arange(tok_rows)[None, :]
    before = jnp.dot(
        earlier.astype(BF16), jnp.any(named, axis=1).astype(BF16), preferred_element_type=F32
    )
    rank = jnp.sum(jnp.where(named, before[:, None, :], 0.0), axis=2).astype(jnp.int32)
    pos = (slot % slots) * rows + (slot // slots) * pad + rank

    vmem = pl.BlockSpec(memory_space=pltpu.VMEM)
    hbm = pl.BlockSpec(memory_space=pl.ANY)
    out = pl.pallas_call(
        functools.partial(kernel, n, ring),
        out_shape=[
            jax.ShapeDtypeStruct((tok_rows, width), BF16),
            jax.ShapeDtypeStruct((tok_rows, width), BF16),
            jax.ShapeDtypeStruct((tok_rows, tops), F32),
            jax.ShapeDtypeStruct((slots, chunk, ff), BF16),
            jax.ShapeDtypeStruct((slots, chunk, ff), BF16),
            jax.ShapeDtypeStruct((slots, ff, chunk), BF16),
            jax.ShapeDtypeStruct((2, slots, n, pad, width), BF16),
            jax.ShapeDtypeStruct((2, slots, 2, chunk, ff), BF16),
            jax.ShapeDtypeStruct((slots, 2, ff, chunk), BF16),
        ],
        in_specs=[vmem] * 6 + [hbm] * 3,
        out_specs=[vmem] * 3 + [hbm] * 6,
        scratch_shapes=[
            pltpu.VMEM((2, slots, n, pad, width), BF16),
            pltpu.VMEM((2, slots, n, pad, width), BF16),
            pltpu.VMEM((width, ff), BF16),
            pltpu.VMEM((width, ff), BF16),
            pltpu.VMEM((ff, width), BF16),
            pltpu.VMEM((2, rows, ff), F32),
            pltpu.VMEM((3, rows, ff), BF16),
            pltpu.VMEM((2, slots, ring, chunk, ff), BF16),
            pltpu.VMEM((slots, ring, ff, chunk), BF16),
            pltpu.VMEM((2, slots, 2, chunk // 2, ff), BF16),
            pltpu.VMEM((slots, 2, ff // 2, chunk), BF16),
            pltpu.VMEM((2, chunk, ff), BF16),
            pltpu.VMEM((2, ff, chunk), BF16),
            pltpu.SemaphoreType.DMA((2, slots)),
            pltpu.SemaphoreType.DMA((2, slots)),
            pltpu.SemaphoreType.DMA((2, slots)),
            pltpu.SemaphoreType.DMA((2, slots)),
            pltpu.SemaphoreType.DMA((3,)),
            pltpu.SemaphoreType.DMA((slots, 3, 3, 2)),
            pltpu.SemaphoreType.DMA((slots, 3, 3, 2)),
            pltpu.SemaphoreType.DMA((2,)),
            pltpu.SemaphoreType.DMA((slots, 3)),
        ],
        compiler_params=pltpu.CompilerParams(
            collective_id=0, has_side_effects=True, vmem_limit_bytes=63 * 1024 * 1024
        ),
    )(pos.T, pos, gate_weights.T, gate_weights, tokens, d_out, w_gate, w_up, w_down)
    return tuple(out[:6])


def solution(mesh):
    token = P(("dp", "expert"), None)
    weight = P("expert", None, None)
    return jax.shard_map(
        functools.partial(on_device, mesh.shape["expert"], mesh.shape["dp"]),
        mesh=mesh,
        in_specs=(token, token, token, P(), weight, weight, weight, token),
        out_specs=(
            token, token, token,
            P("expert", "dp", None), P("expert", "dp", None), P("expert", None, "dp"),
        ),
        check_vma=False,
    )
```

```python
import functools

import jax
import jax.numpy as jnp
from jax import lax
from jax.experimental import pallas as pl
from jax.experimental.pallas import tpu as pltpu
from jax.sharding import PartitionSpec as P

MESH = pl.DeviceIdType.MESH
STRIDE = 3
F32 = jnp.float32
BF16 = jnp.bfloat16
NT = (((1,), (1,)), ((), ()))
TN = (((0,), (0,)), ((), ()))


def mm(a, b):
    return jnp.dot(a, b, preferred_element_type=F32)


def mm_nt(a, b):
    return lax.dot_general(a, b, NT, preferred_element_type=F32)


def mm_tn(a, b):
    return lax.dot_general(a, b, TN, preferred_element_type=F32)


def kernel(
    n, ring, pos_t, pos, gates_t, gates, tok, dout, wg_h, wu_h, wd_h,
    lo, dt, dg, gg, gu, gd, ret, r2w, r2d,
    send, land, wg, wu, wd, act, hid, pw, pd, r1w, r1d, tw, td,
    f_send, f_recv, b_send, b_recv, w_sem, g_send, g_recv, l_sem, o_sem,
):
    me = lax.axis_index("expert")
    r = lax.axis_index("dp")
    right, left, opp = lax.rem(r + 1, ring), lax.rem(r + 3, ring), lax.rem(r + 2, ring)
    slots, _, pad, width = send.shape[1:]
    rows = n * pad
    ff = wg.shape[1]
    chunk = width // ring
    ft = 256
    tops = gates.shape[1]

    barrier = pltpu.get_barrier_semaphore()

    def greet(i, _):
        pl.semaphore_signal(
            barrier, inc=1, device_id={"expert": lax.rem(me + i, n)}, device_id_type=MESH
        )
        return 0

    lax.fori_loop(1, n, greet, 0)
    for side in (right, left):
        pl.semaphore_signal(barrier, inc=1, device_id={"dp": side}, device_id_type=MESH)

    def weight_copies(s):
        return [
            pltpu.make_async_copy(src.at[s], dst, w_sem.at[j])
            for j, (src, dst) in enumerate(((wg_h, wg), (wu_h, wu), (wd_h, wd)))
        ]

    for copy in weight_copies(0):
        copy.start()

    def fill(s):
        spot = lax.broadcasted_iota(jnp.int32, (rows, pos_t.shape[1]), 0) + s * rows
        picked = jnp.zeros(spot.shape, F32)
        weight = jnp.zeros(spot.shape, F32)
        for k in range(tops):
            hit = pos_t[k : k + 1, :] == spot
            picked = jnp.where(hit, 1.0, picked)
            weight = jnp.where(hit, gates_t[k : k + 1, :], weight)
        picked = picked.astype(BF16)
        weight = jnp.sum(weight, axis=1, keepdims=True)

        def tile(j, _):
            cols = pl.ds(pl.multiple_of(j * chunk, chunk), chunk)
            send[0, s, :, :, cols] = mm(picked, tok[:, cols]).astype(BF16).reshape(n, pad, chunk)
            rows_d = mm(picked, dout[:, cols]) * weight
            send[1, s, :, :, cols] = rows_d.astype(BF16).reshape(n, pad, chunk)
            return 0

        lax.fori_loop(0, width // chunk, tile, 0)

    def keep(k, s, dst, r_sem):
        pltpu.make_async_copy(send.at[k, s, me], dst.at[k, s, me], r_sem.at[k, s]).start()

    def row_copy(k, s, peer, dst, s_sem, r_sem):
        return pltpu.make_async_remote_copy(
            src_ref=send.at[k, s, peer],
            dst_ref=dst.at[k, s, me],
            send_sem=s_sem.at[k, s],
            recv_sem=r_sem.at[k, s],
            device_id={"expert": peer},
            device_id_type=MESH,
        )

    def exchange(k, s, dst, s_sem, r_sem):
        keep(k, s, dst, r_sem)

        def go(i, _):
            row_copy(k, s, lax.rem(me + 5 * i, n), dst, s_sem, r_sem).start()
            return 0

        lax.fori_loop(1, n, go, 0)

    def wait_recv(k, s, dst, r_sem):
        pltpu.make_async_copy(dst.at[k, s], dst.at[k, s], r_sem.at[k, s]).wait()

    def wait_send(k, s, s_sem):
        part = send.at[k, s, pl.ds(0, n - 1)]
        pltpu.make_async_copy(part, part, s_sem.at[k, s]).wait()

    items = (
        (pd, r1d, r2d, td, gd),
        (pw.at[0], r1w.at[0], r2w.at[0], tw, gg),
        (pw.at[1], r1w.at[1], r2w.at[1], tw, gu),
    )

    def ring_copy(item, s, step, side):
        part, first, second, _, _ = items[item]
        half = part.shape[2] // 2
        low, high = pl.ds(0, half), pl.ds(half, half)
        near = right if side == 0 else left
        if step == 0:
            rows_s = low if side == 0 else high
            src, dst = part.at[s, opp, rows_s], first.at[s, side]
        else:
            rows_s = (high if side == 0 else low) if step == 1 else (low if side == 0 else high)
            src, dst = part.at[s, near, rows_s], second.at[s, side, rows_s]
        return pltpu.make_async_remote_copy(
            src_ref=src,
            dst_ref=dst,
            send_sem=g_send.at[s, item, step, side],
            recv_sem=g_recv.at[s, item, step, side],
            device_id={"dp": near},
            device_id_type=MESH,
        )

    def ring_start(item, s):
        for step in (0, 1):
            for side in (0, 1):
                ring_copy(item, s, step, side).start()

    def add_rows(dst, src, count):
        block = 64

        def go(j, _):
            at = pl.ds(pl.multiple_of(j * block, block), block)
            dst[at, :] = (dst[at, :].astype(F32) + src[at, :].astype(F32)).astype(BF16)
            return 0

        lax.fori_loop(0, count // block, go, 0)

    def ring_middle(item, s):
        part, first, _, _, _ = items[item]
        half = part.shape[2] // 2
        for side in (0, 1):
            near = right if side == 0 else left
            at = pl.ds(0, half) if side == 0 else pl.ds(half, half)
            ring_copy(item, s, 0, side).wait_recv()
            add_rows(part.at[s, near, at], first.at[s, side], half)
            ring_copy(item, s, 2, side).start()

    def ring_end(item, s):
        part, _, second, temp, out = items[item]
        count = part.shape[2]
        for side in (0, 1):
            for step in (1, 2):
                ring_copy(item, s, step, side).wait_recv()
        loads = [
            pltpu.make_async_copy(second.at[s, side], temp.at[side], l_sem.at[side])
            for side in (0, 1)
        ]
        for copy in loads:
            copy.start()
        for copy in loads:
            copy.wait()
        block = 64
        own = part.at[s, r]

        def go(j, _):
            at = pl.ds(pl.multiple_of(j * block, block), block)
            total = own[at, :].astype(F32) + temp[0, at, :].astype(F32) + temp[1, at, :].astype(F32)
            own[at, :] = total.astype(BF16)
            return 0

        lax.fori_loop(0, count // block, go, 0)
        pltpu.make_async_copy(own, out.at[s], o_sem.at[s, item]).start()

    def rows_of(k, s, cols):
        return land[k, s, :, :, cols].reshape(rows, -1)

    def compute(s, _):
        for copy in weight_copies(s):
            copy.wait()
        wait_recv(0, s, land, f_recv)

        def first(j, _):
            cols = pl.ds(pl.multiple_of(j * ft, ft), ft)
            x = rows_of(0, s, slice(None))
            gate = mm(x, wg[:, cols])
            up = mm(x, wu[:, cols])
            sigma = jax.nn.sigmoid(gate)
            silu = gate * sigma
            hid[0, :, cols] = (silu * up).astype(BF16)
            act[0, :, cols] = up * sigma * (1.0 + gate * (1.0 - sigma))
            act[1, :, cols] = silu
            return 0

        lax.fori_loop(0, ff // ft, first, 0)
        wait_send(0, s, f_send)

        def out_tile(j, _):
            cols = pl.ds(pl.multiple_of(j * chunk, chunk), chunk)
            send[0, s, :, :, cols] = mm(hid[0], wd[:, cols]).astype(BF16).reshape(n, pad, chunk)
            return 0

        lax.fori_loop(0, ring, out_tile, 0)
        exchange(0, s, ret, b_send, b_recv)

        wait_recv(1, s, land, f_recv)

        def down_tile(j, _):
            cols = pl.ds(pl.multiple_of(j * chunk, chunk), chunk)
            pd[s, j] = mm_tn(hid[0], rows_of(1, s, cols)).astype(BF16)
            return 0

        lax.fori_loop(0, ring, down_tile, 0)
        ring_start(0, s)

        def back(j, _):
            cols = pl.ds(pl.multiple_of(j * ft, ft), ft)
            d_hid = mm_nt(rows_of(1, s, slice(None)), wd[cols, :])
            hid[1, :, cols] = (d_hid * act[0, :, cols]).astype(BF16)
            hid[2, :, cols] = (d_hid * act[1, :, cols]).astype(BF16)
            return 0

        lax.fori_loop(0, ff // ft, back, 0)
        for item in (0, 1):

            def up_tile(j, _):
                cols = pl.ds(pl.multiple_of(j * chunk, chunk), chunk)
                pw[item, s, j] = mm_tn(rows_of(0, s, cols), hid[1 + item]).astype(BF16)
                return 0

            lax.fori_loop(0, ring, up_tile, 0)
            ring_start(1 + item, s)
        wait_send(1, s, f_send)

        def in_tile(j, _):
            cols = pl.ds(pl.multiple_of(j * chunk, chunk), chunk)
            total = mm_nt(hid[1], wg[cols, :]) + mm_nt(hid[2], wu[cols, :])
            send[1, s, :, :, cols] = total.astype(BF16).reshape(n, pad, chunk)
            return 0

        lax.fori_loop(0, ring, in_tile, 0)
        exchange(1, s, ret, b_send, b_recv)

        @pl.when(s + 1 < slots)
        def _():
            for copy in weight_copies(s + 1):
                copy.start()

        for item in range(3):
            ring_middle(item, s)
        return 0

    def dispatch(s):
        for k in (0, 1):
            keep(k, s, land, f_recv)
        for core in (0, 1):
            for k in (0, 1):

                def go(i, _):
                    chip = lax.rem(me // 2 + STRIDE * i, n // 2)
                    peer = chip * 2 + core

                    @pl.when(peer != me)
                    def _():
                        row_copy(k, s, peer, land, f_send, f_recv).start()

                    return 0

                lax.fori_loop(0, n // 2, go, 0)

    fill(0)
    pl.semaphore_wait(barrier, n + 1)
    dispatch(0)
    for s in range(1, slots):
        fill(s)
        dispatch(s)
    lax.fori_loop(0, slots, compute, 0)

    for s in range(slots - 1):
        for item in range(3):
            ring_end(item, s)

    spots = slots * rows
    loads = [pltpu.make_async_copy(ret.at[k], land.at[k], l_sem.at[k]) for k in (0, 1)]
    for k in (0, 1):
        for s in range(slots):
            wait_recv(k, s, ret, b_recv)
        loads[k].start()
    spot = lax.broadcasted_iota(jnp.int32, (pos.shape[0], spots), 1)
    hits = [pos[:, k : k + 1] == spot for k in range(tops)]
    hits = [jnp.where(hit, 1.0, 0.0) for hit in hits]
    whole = sum(hits).astype(BF16)
    hits = [hit.astype(BF16) for hit in hits]
    for copy in loads:
        copy.wait()

    def combine(j, sums):
        cols = pl.ds(pl.multiple_of(j * chunk, chunk), chunk)
        outs = land[0, :, :, :, cols].reshape(spots, chunk)
        d_ins = land[1, :, :, :, cols].reshape(spots, chunk)
        d_here = dout[:, cols].astype(F32)
        layer = jnp.zeros(d_here.shape, F32)
        result = []
        for k in range(tops):
            got = mm(hits[k], outs)
            layer = layer + gates[:, k : k + 1] * got
            result.append(sums[k] + jnp.sum(d_here * got, axis=1, keepdims=True))
        lo[:, cols] = layer.astype(BF16)
        dt[:, cols] = mm(whole, d_ins).astype(BF16)
        return tuple(result)

    zero = jnp.zeros((pos.shape[0], 1), F32)
    sums = lax.fori_loop(0, ring, combine, (zero,) * tops)
    for k in range(tops):
        dg[:, k : k + 1] = sums[k]

    for item in range(3):
        ring_end(item, slots - 1)
    for s in range(slots):
        for item in range(3):
            part, _, _, _, out = items[item]
            pltpu.make_async_copy(part.at[s, r], out.at[s], o_sem.at[s, item]).wait()
            for step in range(3):
                for side in (0, 1):
                    ring_copy(item, s, step, side).wait_send()
        for k in (0, 1):
            wait_send(k, s, b_send)


def on_device(n, ring, tokens, expert_ids, gate_weights, slot_of_expert, w_gate, w_up, w_down, d_out):
    slots, width, ff = w_gate.shape
    tok_rows, tops = expert_ids.shape
    experts = slots * n
    capacity = tok_rows * tops * 7 // (4 * experts)
    pad = -(-capacity // 16) * 16
    rows = n * pad
    chunk = width // ring

    wide = jnp.arange(experts, dtype=jnp.int32)
    slot = jnp.sum(jnp.where(expert_ids[:, :, None] == wide, slot_of_expert, 0), axis=2)
    named = slot[:, :, None] == wide
    earlier = jnp.arange(tok_rows)[:, None] > jnp.arange(tok_rows)[None, :]
    before = jnp.dot(
        earlier.astype(BF16), jnp.any(named, axis=1).astype(BF16), preferred_element_type=F32
    )
    rank = jnp.sum(jnp.where(named, before[:, None, :], 0.0), axis=2).astype(jnp.int32)
    pos = (slot % slots) * rows + (slot // slots) * pad + rank

    vmem = pl.BlockSpec(memory_space=pltpu.VMEM)
    hbm = pl.BlockSpec(memory_space=pl.ANY)
    out = pl.pallas_call(
        functools.partial(kernel, n, ring),
        out_shape=[
            jax.ShapeDtypeStruct((tok_rows, width), BF16),
            jax.ShapeDtypeStruct((tok_rows, width), BF16),
            jax.ShapeDtypeStruct((tok_rows, tops), F32),
            jax.ShapeDtypeStruct((slots, chunk, ff), BF16),
            jax.ShapeDtypeStruct((slots, chunk, ff), BF16),
            jax.ShapeDtypeStruct((slots, ff, chunk), BF16),
            jax.ShapeDtypeStruct((2, slots, n, pad, width), BF16),
            jax.ShapeDtypeStruct((2, slots, 2, chunk, ff), BF16),
            jax.ShapeDtypeStruct((slots, 2, ff, chunk), BF16),
        ],
        in_specs=[vmem] * 6 + [hbm] * 3,
        out_specs=[vmem] * 3 + [hbm] * 6,
        scratch_shapes=[
            pltpu.VMEM((2, slots, n, pad, width), BF16),
            pltpu.VMEM((2, slots, n, pad, width), BF16),
            pltpu.VMEM((width, ff), BF16),
            pltpu.VMEM((width, ff), BF16),
            pltpu.VMEM((ff, width), BF16),
            pltpu.VMEM((2, rows, ff), F32),
            pltpu.VMEM((3, rows, ff), BF16),
            pltpu.VMEM((2, slots, ring, chunk, ff), BF16),
            pltpu.VMEM((slots, ring, ff, chunk), BF16),
            pltpu.VMEM((2, slots, 2, chunk // 2, ff), BF16),
            pltpu.VMEM((slots, 2, ff // 2, chunk), BF16),
            pltpu.VMEM((2, chunk, ff), BF16),
            pltpu.VMEM((2, ff, chunk), BF16),
            pltpu.SemaphoreType.DMA((2, slots)),
            pltpu.SemaphoreType.DMA((2, slots)),
            pltpu.SemaphoreType.DMA((2, slots)),
            pltpu.SemaphoreType.DMA((2, slots)),
            pltpu.SemaphoreType.DMA((3,)),
            pltpu.SemaphoreType.DMA((slots, 3, 3, 2)),
            pltpu.SemaphoreType.DMA((slots, 3, 3, 2)),
            pltpu.SemaphoreType.DMA((2,)),
            pltpu.SemaphoreType.DMA((slots, 3)),
        ],
        compiler_params=pltpu.CompilerParams(
            collective_id=0, has_side_effects=True, vmem_limit_bytes=63 * 1024 * 1024
        ),
    )(pos.T, pos, gate_weights.T, gate_weights, tokens, d_out, w_gate, w_up, w_down)
    return tuple(out[:6])


def solution(mesh):
    token = P(("dp", "expert"), None)
    weight = P("expert", None, None)
    return jax.shard_map(
        functools.partial(on_device, mesh.shape["expert"], mesh.shape["dp"]),
        mesh=mesh,
        in_specs=(token, token, token, P(), weight, weight, weight, token),
        out_specs=(
            token, token, token,
            P("expert", "dp", None), P("expert", "dp", None), P("expert", None, "dp"),
        ),
        check_vma=False,
    )
```

```python
import functools

import jax
import jax.numpy as jnp
from jax import lax
from jax.experimental import pallas as pl
from jax.experimental.pallas import tpu as pltpu
from jax.sharding import PartitionSpec as P

MESH = pl.DeviceIdType.MESH
STRIDE = 3
F32 = jnp.float32
BF16 = jnp.bfloat16
NT = (((1,), (1,)), ((), ()))
TN = (((0,), (0,)), ((), ()))


def mm(a, b):
    return jnp.dot(a, b, preferred_element_type=F32)


def mm_nt(a, b):
    return lax.dot_general(a, b, NT, preferred_element_type=F32)


def mm_tn(a, b):
    return lax.dot_general(a, b, TN, preferred_element_type=F32)


def kernel(
    n, ring, gates_pos, tok, dout, wg_h, wu_h, wd_h,
    lo, dt, dg, own_w, own_d, ret, r2w, r2d,
    send, land, wg, wu, wd, act, hid, pw, pd, r1w, r1d,
    f_send, f_recv, b_send, b_recv, w_sem, g_send, g_recv, l_sem, o_sem,
):
    me = lax.axis_index("expert")
    r = lax.axis_index("dp")
    right, left, opp = lax.rem(r + 1, ring), lax.rem(r + 3, ring), lax.rem(r + 2, ring)
    slots, _, pad, width = send.shape[1:]
    rows = n * pad
    ff = wg.shape[1]
    chunk = width // ring
    ft = 256
    tops = gates_pos.shape[0] // 2
    tok_rows = tok.shape[0]

    barrier = pltpu.get_barrier_semaphore()

    def greet(i, _):
        pl.semaphore_signal(
            barrier, inc=1, device_id={"expert": lax.rem(me + i, n)}, device_id_type=MESH
        )
        return 0

    lax.fori_loop(1, n, greet, 0)
    for side in (right, left):
        pl.semaphore_signal(barrier, inc=1, device_id={"dp": side}, device_id_type=MESH)

    def weight_copies(s):
        return [
            pltpu.make_async_copy(src.at[s], dst, w_sem.at[j])
            for j, (src, dst) in enumerate(((wg_h, wg), (wu_h, wu), (wd_h, wd)))
        ]

    for copy in weight_copies(0):
        copy.start()

    def fill(s):
        spot = lax.broadcasted_iota(jnp.int32, (rows, tok_rows), 0) + s * rows
        picked = jnp.zeros(spot.shape, F32)
        weight = jnp.zeros(spot.shape, F32)
        for k in range(tops):
            hit = gates_pos[tops + k : tops + k + 1, :].astype(jnp.int32) == spot
            picked = jnp.where(hit, 1.0, picked)
            weight = jnp.where(hit, gates_pos[k : k + 1, :], weight)
        picked = picked.astype(BF16)
        weight = jnp.sum(weight, axis=1, keepdims=True)

        def tile(j, _):
            cols = pl.ds(pl.multiple_of(j * chunk, chunk), chunk)
            send[0, s, :, :, cols] = mm(picked, tok[:, cols]).astype(BF16).reshape(n, pad, chunk)
            rows_d = mm(picked, dout[:, cols]) * weight
            send[1, s, :, :, cols] = rows_d.astype(BF16).reshape(n, pad, chunk)
            return 0

        lax.fori_loop(0, width // chunk, tile, 0)

    def keep(k, s, dst, r_sem):
        pltpu.make_async_copy(send.at[k, s, me], dst.at[k, s, me], r_sem.at[k, s]).start()

    def row_copy(k, s, peer, dst, s_sem, r_sem):
        return pltpu.make_async_remote_copy(
            src_ref=send.at[k, s, peer],
            dst_ref=dst.at[k, s, me],
            send_sem=s_sem.at[k, s],
            recv_sem=r_sem.at[k, s],
            device_id={"expert": peer},
            device_id_type=MESH,
        )

    def exchange(k, s, dst, s_sem, r_sem):
        keep(k, s, dst, r_sem)

        def go(i, _):
            row_copy(k, s, lax.rem(me + 5 * i, n), dst, s_sem, r_sem).start()
            return 0

        lax.fori_loop(1, n, go, 0)

    def wait_recv(k, s, dst, r_sem):
        pltpu.make_async_copy(dst.at[k, s], dst.at[k, s], r_sem.at[k, s]).wait()

    def wait_send(k, s, s_sem):
        part = send.at[k, s, pl.ds(0, n - 1)]
        pltpu.make_async_copy(part, part, s_sem.at[k, s]).wait()

    items = (
        (pd, r1d, r2d, own_d),
        (pw.at[0], r1w.at[0], r2w.at[0], own_w.at[0]),
        (pw.at[1], r1w.at[1], r2w.at[1], own_w.at[1]),
    )

    def ring_copy(item, s, step, side):
        part, first, second, _ = items[item]
        half = part.shape[2] // 2
        low, high = pl.ds(0, half), pl.ds(half, half)
        near = right if side == 0 else left
        if step == 0:
            rows_s = low if side == 0 else high
            src, dst = part.at[s, opp, rows_s], first.at[s, side]
        else:
            rows_s = (high if side == 0 else low) if step == 1 else (low if side == 0 else high)
            src, dst = part.at[s, near, rows_s], second.at[side, s, rows_s]
        return pltpu.make_async_remote_copy(
            src_ref=src,
            dst_ref=dst,
            send_sem=g_send.at[s, item, step, side],
            recv_sem=g_recv.at[s, item, step, side],
            device_id={"dp": near},
            device_id_type=MESH,
        )

    def ring_start(item, s):
        for step in (0, 1):
            for side in (0, 1):
                ring_copy(item, s, step, side).start()

    def add_rows(dst, src, count):
        block = 64

        def go(j, _):
            at = pl.ds(pl.multiple_of(j * block, block), block)
            dst[at, :] = (dst[at, :].astype(F32) + src[at, :].astype(F32)).astype(BF16)
            return 0

        lax.fori_loop(0, count // block, go, 0)

    def ring_middle(item, s):
        part, first, _, _ = items[item]
        half = part.shape[2] // 2
        for side in (0, 1):
            near = right if side == 0 else left
            at = pl.ds(0, half) if side == 0 else pl.ds(half, half)
            ring_copy(item, s, 0, side).wait_recv()
            add_rows(part.at[s, near, at], first.at[s, side], half)
            ring_copy(item, s, 2, side).start()

    def own_copy(item, s):
        part, _, _, own = items[item]
        return pltpu.make_async_copy(part.at[s, r], own.at[s], o_sem.at[s, item])

    def rows_of(k, s, cols):
        return land[k, s, :, :, cols].reshape(rows, -1)

    def compute(s, _):
        for copy in weight_copies(s):
            copy.wait()
        wait_recv(0, s, land, f_recv)

        def first(j, _):
            cols = pl.ds(pl.multiple_of(j * ft, ft), ft)
            x = rows_of(0, s, slice(None))
            gate = mm(x, wg[:, cols])
            up = mm(x, wu[:, cols])
            sigma = jax.nn.sigmoid(gate)
            silu = gate * sigma
            hid[0, :, cols] = (silu * up).astype(BF16)
            act[0, :, cols] = up * sigma * (1.0 + gate * (1.0 - sigma))
            act[1, :, cols] = silu
            return 0

        lax.fori_loop(0, ff // ft, first, 0)
        wait_send(0, s, f_send)

        def out_tile(j, _):
            cols = pl.ds(pl.multiple_of(j * chunk, chunk), chunk)
            send[0, s, :, :, cols] = mm(hid[0], wd[:, cols]).astype(BF16).reshape(n, pad, chunk)
            return 0

        lax.fori_loop(0, ring, out_tile, 0)
        exchange(0, s, ret, b_send, b_recv)

        wait_recv(1, s, land, f_recv)

        def down_tile(j, _):
            at = lax.rem(opp + j, ring)
            cols = pl.ds(pl.multiple_of(at * chunk, chunk), chunk)
            pd[s, at] = mm_tn(hid[0], rows_of(1, s, cols)).astype(BF16)

            @pl.when(j == 0)
            def _():
                for side in (0, 1):
                    ring_copy(0, s, 0, side).start()

            return 0

        lax.fori_loop(0, ring, down_tile, 0)
        for side in (0, 1):
            ring_copy(0, s, 1, side).start()
        own_copy(0, s).start()

        def back(j, _):
            cols = pl.ds(pl.multiple_of(j * ft, ft), ft)
            d_hid = mm_nt(rows_of(1, s, slice(None)), wd[cols, :])
            hid[1, :, cols] = (d_hid * act[0, :, cols]).astype(BF16)
            hid[2, :, cols] = (d_hid * act[1, :, cols]).astype(BF16)
            return 0

        lax.fori_loop(0, ff // ft, back, 0)
        for item in (0, 1):

            def up_tile(j, _):
                cols = pl.ds(pl.multiple_of(j * chunk, chunk), chunk)
                pw[item, s, j] = mm_tn(rows_of(0, s, cols), hid[1 + item]).astype(BF16)
                return 0

            lax.fori_loop(0, ring, up_tile, 0)
            ring_start(1 + item, s)
            own_copy(1 + item, s).start()
        wait_send(1, s, f_send)

        def in_tile(j, _):
            cols = pl.ds(pl.multiple_of(j * chunk, chunk), chunk)
            total = mm_nt(hid[1], wg[cols, :]) + mm_nt(hid[2], wu[cols, :])
            send[1, s, :, :, cols] = total.astype(BF16).reshape(n, pad, chunk)
            return 0

        lax.fori_loop(0, ring, in_tile, 0)
        exchange(1, s, ret, b_send, b_recv)

        @pl.when(s + 1 < slots)
        def _():
            for copy in weight_copies(s + 1):
                copy.start()

        for item in range(3):
            ring_middle(item, s)
        return 0

    def dispatch(s):
        for k in (0, 1):
            keep(k, s, land, f_recv)
        for core in (0, 1):
            for k in (0, 1):

                def go(i, _):
                    chip = lax.rem(me // 2 + STRIDE * i, n // 2)
                    peer = chip * 2 + core

                    @pl.when(peer != me)
                    def _():
                        row_copy(k, s, peer, land, f_send, f_recv).start()

                    return 0

                lax.fori_loop(0, n // 2, go, 0)

    fill(0)
    pl.semaphore_wait(barrier, n + 1)
    dispatch(0)
    for s in range(1, slots):
        fill(s)
        dispatch(s)
    lax.fori_loop(0, slots, compute, 0)

    spots = slots * rows
    spot = lax.broadcasted_iota(jnp.int32, (tok_rows, spots), 1)
    columns = gates_pos[...].T
    hits = [columns[:, tops + k : tops + k + 1].astype(jnp.int32) == spot for k in range(tops)]
    hits = [jnp.where(hit, 1.0, 0.0) for hit in hits]
    whole = sum(hits).astype(BF16)
    hits = [hit.astype(BF16) for hit in hits]

    def fetch(k):
        loads = [
            pltpu.make_async_copy(ret.at[k, s], land.at[k, s], l_sem.at[k, s]) for s in range(slots)
        ]
        for s in range(slots):
            wait_recv(k, s, ret, b_recv)
            loads[s].start()
        for s in range(slots):
            loads[s].wait()

    fetch(0)

    def combine(j, sums):
        cols = pl.ds(pl.multiple_of(j * chunk, chunk), chunk)
        outs = land[0, :, :, :, cols].reshape(spots, chunk)
        d_here = dout[:, cols].astype(F32)
        layer = jnp.zeros(d_here.shape, F32)
        result = []
        for k in range(tops):
            got = mm(hits[k], outs)
            layer = layer + columns[:, k : k + 1] * got
            result.append(sums[k] + jnp.sum(d_here * got, axis=1, keepdims=True))
        lo[:, cols] = layer.astype(BF16)
        return tuple(result)

    zero = jnp.zeros((tok_rows, 1), F32)
    sums = lax.fori_loop(0, ring, combine, (zero,) * tops)
    lane = lax.broadcasted_iota(jnp.int32, (tok_rows, 128), 1)
    table = jnp.zeros(lane.shape, F32)
    for k in range(tops):
        table = jnp.where(lane == k, sums[k], table)
    dg[...] = table.T[:tops]

    fetch(1)

    def combine_in(j, _):
        cols = pl.ds(pl.multiple_of(j * chunk, chunk), chunk)
        dt[:, cols] = mm(whole, land[1, :, :, :, cols].reshape(spots, chunk)).astype(BF16)
        return 0

    lax.fori_loop(0, ring, combine_in, 0)

    for s in range(slots):
        for item in range(3):
            own_copy(item, s).wait()
            for side in (0, 1):
                for step in (1, 2):
                    ring_copy(item, s, step, side).wait_recv()
                for step in range(3):
                    ring_copy(item, s, step, side).wait_send()
        for k in (0, 1):
            wait_send(k, s, b_send)


def on_device(n, ring, tokens, expert_ids, gate_weights, slot_of_expert, w_gate, w_up, w_down, d_out):
    slots, width, ff = w_gate.shape
    tok_rows, tops = expert_ids.shape
    experts = slots * n
    capacity = tok_rows * tops * 7 // (4 * experts)
    pad = -(-capacity // 16) * 16
    rows = n * pad
    chunk = width // ring

    wide = jnp.arange(experts, dtype=jnp.int32)
    slot = jnp.sum(jnp.where(expert_ids[:, :, None] == wide, slot_of_expert, 0), axis=2)
    named = slot[:, :, None] == wide
    earlier = jnp.arange(tok_rows)[:, None] > jnp.arange(tok_rows)[None, :]
    before = jnp.dot(
        earlier.astype(BF16), jnp.any(named, axis=1).astype(BF16), preferred_element_type=F32
    )
    rank = jnp.sum(jnp.where(named, before[:, None, :], 0.0), axis=2).astype(jnp.int32)
    pos = (slot % slots) * rows + (slot // slots) * pad + rank

    vmem = pl.BlockSpec(memory_space=pltpu.VMEM)
    hbm = pl.BlockSpec(memory_space=pl.ANY)
    gates_pos = jnp.concatenate([gate_weights.T, pos.T.astype(F32)], axis=0)
    out = pl.pallas_call(
        functools.partial(kernel, n, ring),
        out_shape=[
            jax.ShapeDtypeStruct((tok_rows, width), BF16),
            jax.ShapeDtypeStruct((tok_rows, width), BF16),
            jax.ShapeDtypeStruct((tops, tok_rows), F32),
            jax.ShapeDtypeStruct((2, slots, chunk, ff), BF16),
            jax.ShapeDtypeStruct((slots, ff, chunk), BF16),
            jax.ShapeDtypeStruct((2, slots, n, pad, width), BF16),
            jax.ShapeDtypeStruct((2, 2, slots, chunk, ff), BF16),
            jax.ShapeDtypeStruct((2, slots, ff, chunk), BF16),
        ],
        in_specs=[vmem] * 3 + [hbm] * 3,
        out_specs=[vmem] * 3 + [hbm] * 5,
        scratch_shapes=[
            pltpu.VMEM((2, slots, n, pad, width), BF16),
            pltpu.VMEM((2, slots, n, pad, width), BF16),
            pltpu.VMEM((width, ff), BF16),
            pltpu.VMEM((width, ff), BF16),
            pltpu.VMEM((ff, width), BF16),
            pltpu.VMEM((2, rows, ff), F32),
            pltpu.VMEM((3, rows, ff), BF16),
            pltpu.VMEM((2, slots, ring, chunk, ff), BF16),
            pltpu.VMEM((slots, ring, ff, chunk), BF16),
            pltpu.VMEM((2, slots, 2, chunk // 2, ff), BF16),
            pltpu.VMEM((slots, 2, ff // 2, chunk), BF16),
            pltpu.SemaphoreType.DMA((2, slots)),
            pltpu.SemaphoreType.DMA((2, slots)),
            pltpu.SemaphoreType.DMA((2, slots)),
            pltpu.SemaphoreType.DMA((2, slots)),
            pltpu.SemaphoreType.DMA((3,)),
            pltpu.SemaphoreType.DMA((slots, 3, 3, 2)),
            pltpu.SemaphoreType.DMA((slots, 3, 3, 2)),
            pltpu.SemaphoreType.DMA((2, slots)),
            pltpu.SemaphoreType.DMA((slots, 3)),
        ],
        compiler_params=pltpu.CompilerParams(
            collective_id=0, has_side_effects=True, vmem_limit_bytes=63 * 1024 * 1024
        ),
    )(gates_pos, tokens, d_out, w_gate, w_up, w_down)
    layer_out, d_tokens, d_gates, own_w, own_d, _, got_w, got_d = out

    def total(own, got):
        return (own.astype(F32) + got[0].astype(F32) + got[1].astype(F32)).astype(BF16)

    return (
        layer_out, d_tokens, d_gates.T,
        total(own_w[0], got_w[0]), total(own_w[1], got_w[1]), total(own_d, got_d),
    )


def solution(mesh):
    token = P(("dp", "expert"), None)
    weight = P("expert", None, None)
    return jax.shard_map(
        functools.partial(on_device, mesh.shape["expert"], mesh.shape["dp"]),
        mesh=mesh,
        in_specs=(token, token, token, P(), weight, weight, weight, token),
        out_specs=(
            token, token, token,
            P("expert", "dp", None), P("expert", "dp", None), P("expert", None, "dp"),
        ),
        check_vma=False,
    )
```

```python
import functools

import jax
import jax.numpy as jnp
from jax import lax
from jax.experimental import pallas as pl
from jax.experimental.pallas import tpu as pltpu
from jax.sharding import PartitionSpec as P

MESH = pl.DeviceIdType.MESH
STRIDE = 3
FORWARD_AT = (1, 1, 1, 1)
RETURN_AT = (1, 1, 2, 3)
LAST_AT = (0, 0, 0, 0)
F32 = jnp.float32
BF16 = jnp.bfloat16
NT = (((1,), (1,)), ((), ()))
TN = (((0,), (0,)), ((), ()))


def mm(a, b):
    return jnp.dot(a, b, preferred_element_type=F32)


def mm_nt(a, b):
    return lax.dot_general(a, b, NT, preferred_element_type=F32)


def mm_tn(a, b):
    return lax.dot_general(a, b, TN, preferred_element_type=F32)


def kernel(
    n, ring, gates_pos, tok, dout, wg_h, wu_h, wd_h,
    lo, dt, dg, own_w, own_d, ret, r2w, r2d,
    send, land, wg, wu, wd, act, hid, pw, pd, r1w, r1d, tw, td,
    f_send, f_recv, b_send, b_recv, w_sem, g_send, g_recv, l_sem, o_sem, t_sem,
):
    me = lax.axis_index("expert")
    r = lax.axis_index("dp")
    right, left, opp = lax.rem(r + 1, ring), lax.rem(r + 3, ring), lax.rem(r + 2, ring)
    slots, _, pad, width = send.shape[1:]
    rows = n * pad
    ff = wg.shape[1]
    chunk = width // ring
    ft = 256
    tops = gates_pos.shape[0] // 2
    tok_rows = tok.shape[0]

    barrier = pltpu.get_barrier_semaphore()

    def greet(i, _):
        pl.semaphore_signal(
            barrier, inc=1, device_id={"expert": lax.rem(me + i, n)}, device_id_type=MESH
        )
        return 0

    lax.fori_loop(1, n, greet, 0)
    for side in (right, left):
        pl.semaphore_signal(barrier, inc=1, device_id={"dp": side}, device_id_type=MESH)

    def weight_copies(s):
        return [
            pltpu.make_async_copy(src.at[s], dst, w_sem.at[j])
            for j, (src, dst) in enumerate(((wg_h, wg), (wu_h, wu), (wd_h, wd)))
        ]

    for copy in weight_copies(0):
        copy.start()

    def fill(s):
        spot = lax.broadcasted_iota(jnp.int32, (rows, tok_rows), 0) + s * rows
        picked = jnp.zeros(spot.shape, F32)
        weight = jnp.zeros(spot.shape, F32)
        for k in range(tops):
            hit = gates_pos[tops + k : tops + k + 1, :].astype(jnp.int32) == spot
            picked = jnp.where(hit, 1.0, picked)
            weight = jnp.where(hit, gates_pos[k : k + 1, :], weight)
        picked = picked.astype(BF16)
        weight = jnp.sum(weight, axis=1, keepdims=True)

        def tile(j, _):
            cols = pl.ds(pl.multiple_of(j * chunk, chunk), chunk)
            send[0, s, :, :, cols] = mm(picked, tok[:, cols]).astype(BF16).reshape(n, pad, chunk)
            rows_d = mm(picked, dout[:, cols]) * weight
            send[1, s, :, :, cols] = rows_d.astype(BF16).reshape(n, pad, chunk)
            return 0

        lax.fori_loop(0, width // chunk, tile, 0)

    def keep(k, s, dst, r_sem):
        pltpu.make_async_copy(send.at[k, s, me], dst.at[k, s, me], r_sem.at[k, s]).start()

    def row_copy(k, s, peer, dst, s_sem, r_sem):
        return pltpu.make_async_remote_copy(
            src_ref=send.at[k, s, peer],
            dst_ref=dst.at[k, s, me],
            send_sem=s_sem.at[k, s],
            recv_sem=r_sem.at[k, s],
            device_id={"expert": peer},
            device_id_type=MESH,
        )

    def send_part(k, s, core, dst, s_sem, r_sem):
        def go(i, _):
            chip = lax.rem(me // 2 + STRIDE * i, n // 2)
            peer = chip * 2 + core

            @pl.when(peer != me)
            def _():
                row_copy(k, s, peer, dst, s_sem, r_sem).start()

            return 0

        if core == 0:
            keep(k, s, dst, r_sem)
        lax.fori_loop(0, n // 2, go, 0)

    def forward_part(q, s):
        send_part(q % 2, s, q // 2, land, f_send, f_recv)

    def return_part(q, s):
        send_part(q // 2, s, q % 2, ret, b_send, b_recv)

    def next_parts(point, s):
        @pl.when(s + 1 < slots)
        def _():
            for q in range(4):
                if FORWARD_AT[q] == point:
                    forward_part(q, s + 1)

        @pl.when(s > 0)
        def _():
            for q in range(4):
                if RETURN_AT[q] == point:
                    return_part(q, s - 1)

    def wait_recv(k, s, dst, r_sem):
        pltpu.make_async_copy(dst.at[k, s], dst.at[k, s], r_sem.at[k, s]).wait()

    def wait_send(k, s, s_sem):
        part = send.at[k, s, pl.ds(0, n - 1)]
        pltpu.make_async_copy(part, part, s_sem.at[k, s]).wait()

    items = (
        (pd, r1d, r2d, own_d, td),
        (pw.at[0], r1w.at[0], r2w.at[0], own_w.at[0], tw),
        (pw.at[1], r1w.at[1], r2w.at[1], own_w.at[1], tw),
    )

    def ring_copy(item, s, step, side):
        part, first, second, _, _ = items[item]
        half = part.shape[2] // 2
        low, high = pl.ds(0, half), pl.ds(half, half)
        near = right if side == 0 else left
        if step == 0:
            rows_s = low if side == 0 else high
            src, dst = part.at[s, opp, rows_s], first.at[s, side]
        else:
            rows_s = (high if side == 0 else low) if step == 1 else (low if side == 0 else high)
            src, dst = part.at[s, near, rows_s], second.at[side, s, rows_s]
        return pltpu.make_async_remote_copy(
            src_ref=src,
            dst_ref=dst,
            send_sem=g_send.at[s, item, step, side],
            recv_sem=g_recv.at[s, item, step, side],
            device_id={"dp": near},
            device_id_type=MESH,
        )

    def ring_start(item, s):
        for step in (0, 1):
            for side in (0, 1):
                ring_copy(item, s, step, side).start()

    def add_rows(dst, src, count):
        block = 64

        def go(j, _):
            at = pl.ds(pl.multiple_of(j * block, block), block)
            dst[at, :] = (dst[at, :].astype(F32) + src[at, :].astype(F32)).astype(BF16)
            return 0

        lax.fori_loop(0, count // block, go, 0)

    def ring_middle(item, s):
        part, first, _, _, _ = items[item]
        half = part.shape[2] // 2
        for side in (0, 1):
            near = right if side == 0 else left
            at = pl.ds(0, half) if side == 0 else pl.ds(half, half)
            ring_copy(item, s, 0, side).wait_recv()
            add_rows(part.at[s, near, at], first.at[s, side], half)
            ring_copy(item, s, 2, side).start()

    def own_copy(item, s):
        part, _, _, own, _ = items[item]
        return pltpu.make_async_copy(part.at[s, r], own.at[s], o_sem.at[s, item])

    def ring_end(item, s):
        part, _, second, _, temp = items[item]
        loads = [
            pltpu.make_async_copy(second.at[side, s], temp.at[side], t_sem.at[side])
            for side in (0, 1)
        ]
        for side in (0, 1):
            for step in (1, 2):
                ring_copy(item, s, step, side).wait_recv()
            loads[side].start()
        for copy in loads:
            copy.wait()
        block = 64
        total = part.at[s, r]

        def go(j, _):
            at = pl.ds(pl.multiple_of(j * block, block), block)
            both = temp[0, at, :].astype(F32) + temp[1, at, :].astype(F32)
            total[at, :] = (total[at, :].astype(F32) + both).astype(BF16)
            return 0

        lax.fori_loop(0, part.shape[2] // block, go, 0)
        own_copy(item, s).start()

    def rows_of(k, s, cols):
        return land[k, s, :, :, cols].reshape(rows, -1)

    def compute(s, _):
        for copy in weight_copies(s):
            copy.wait()
        wait_recv(0, s, land, f_recv)

        def first(j, _):
            cols = pl.ds(pl.multiple_of(j * ft, ft), ft)
            x = rows_of(0, s, slice(None))
            gate = mm(x, wg[:, cols])
            up = mm(x, wu[:, cols])
            sigma = jax.nn.sigmoid(gate)
            silu = gate * sigma
            hid[0, :, cols] = (silu * up).astype(BF16)
            act[0, :, cols] = up * sigma * (1.0 + gate * (1.0 - sigma))
            act[1, :, cols] = silu
            return 0

        lax.fori_loop(0, ff // ft, first, 0)
        wait_send(0, s, f_send)

        def out_tile(j, _):
            cols = pl.ds(pl.multiple_of(j * chunk, chunk), chunk)
            send[0, s, :, :, cols] = mm(hid[0], wd[:, cols]).astype(BF16).reshape(n, pad, chunk)
            return 0

        lax.fori_loop(0, ring, out_tile, 0)
        next_parts(0, s)
        wait_recv(1, s, land, f_recv)

        def down_tile(j, _):
            at = lax.rem(opp + j, ring)
            cols = pl.ds(pl.multiple_of(at * chunk, chunk), chunk)
            pd[s, at] = mm_tn(hid[0], rows_of(1, s, cols)).astype(BF16)

            @pl.when(j == 0)
            def _():
                for side in (0, 1):
                    ring_copy(0, s, 0, side).start()

            return 0

        lax.fori_loop(0, ring, down_tile, 0)
        for side in (0, 1):
            ring_copy(0, s, 1, side).start()
        @pl.when(s == slots - 1)
        def _():
            own_copy(0, s).start()

        next_parts(1, s)

        def back(j, _):
            cols = pl.ds(pl.multiple_of(j * ft, ft), ft)
            d_hid = mm_nt(rows_of(1, s, slice(None)), wd[cols, :])
            hid[1, :, cols] = (d_hid * act[0, :, cols]).astype(BF16)
            hid[2, :, cols] = (d_hid * act[1, :, cols]).astype(BF16)
            return 0

        lax.fori_loop(0, ff // ft, back, 0)
        for item in (0, 1):

            def up_tile(j, _):
                cols = pl.ds(pl.multiple_of(j * chunk, chunk), chunk)
                pw[item, s, j] = mm_tn(rows_of(0, s, cols), hid[1 + item]).astype(BF16)
                return 0

            lax.fori_loop(0, ring, up_tile, 0)
            ring_start(1 + item, s)

            @pl.when(s == slots - 1)
            def _():
                own_copy(1 + item, s).start()

            next_parts(2 + item, s)
        wait_send(1, s, f_send)

        def in_tile(j, _):
            cols = pl.ds(pl.multiple_of(j * chunk, chunk), chunk)
            total = mm_nt(hid[1], wg[cols, :]) + mm_nt(hid[2], wu[cols, :])
            send[1, s, :, :, cols] = total.astype(BF16).reshape(n, pad, chunk)
            return 0

        lax.fori_loop(0, ring, in_tile, 0)
        @pl.when(s + 1 < slots)
        def _():
            for copy in weight_copies(s + 1):
                copy.start()

        for q in range(4):

            @pl.when(s == slots - 1)
            def _():
                for part in range(4):
                    if LAST_AT[part] == q:
                        return_part(part, s)

            if q < 3:
                ring_middle(q, s)
        return 0

    fill(0)
    pl.semaphore_wait(barrier, n + 1)
    for q in range(4):
        forward_part(q, 0)
    for s in range(1, slots):
        fill(s)
    lax.fori_loop(0, slots, compute, 0)

    spots = slots * rows
    spot = lax.broadcasted_iota(jnp.int32, (tok_rows, spots), 1)
    columns = gates_pos[...].T
    hits = [columns[:, tops + k : tops + k + 1].astype(jnp.int32) == spot for k in range(tops)]
    hits = [jnp.where(hit, 1.0, 0.0) for hit in hits]
    whole = sum(hits).astype(BF16)
    hits = [hit.astype(BF16) for hit in hits]

    def fetch(k):
        loads = [
            pltpu.make_async_copy(ret.at[k, s], land.at[k, s], l_sem.at[k, s]) for s in range(slots)
        ]
        for s in range(slots):
            wait_recv(k, s, ret, b_recv)
            loads[s].start()
        for s in range(slots):
            loads[s].wait()

    for s in range(slots - 1):
        for item in range(3):
            ring_end(item, s)
    fetch(0)

    def combine(j, sums):
        cols = pl.ds(pl.multiple_of(j * chunk, chunk), chunk)
        outs = land[0, :, :, :, cols].reshape(spots, chunk)
        d_here = dout[:, cols].astype(F32)
        layer = jnp.zeros(d_here.shape, F32)
        result = []
        for k in range(tops):
            got = mm(hits[k], outs)
            layer = layer + columns[:, k : k + 1] * got
            result.append(sums[k] + jnp.sum(d_here * got, axis=1, keepdims=True))
        lo[:, cols] = layer.astype(BF16)
        return tuple(result)

    zero = jnp.zeros((tok_rows, 1), F32)
    sums = lax.fori_loop(0, ring, combine, (zero,) * tops)
    lane = lax.broadcasted_iota(jnp.int32, (tok_rows, 128), 1)
    table = jnp.zeros(lane.shape, F32)
    for k in range(tops):
        table = jnp.where(lane == k, sums[k], table)
    dg[...] = table.T[:tops]

    fetch(1)

    def combine_in(j, _):
        cols = pl.ds(pl.multiple_of(j * chunk, chunk), chunk)
        dt[:, cols] = mm(whole, land[1, :, :, :, cols].reshape(spots, chunk)).astype(BF16)
        return 0

    lax.fori_loop(0, ring, combine_in, 0)

    for s in range(slots):
        for item in range(3):
            own_copy(item, s).wait()
            for side in (0, 1):
                if s == slots - 1:
                    for step in (1, 2):
                        ring_copy(item, s, step, side).wait_recv()
                for step in range(3):
                    ring_copy(item, s, step, side).wait_send()
        for k in (0, 1):
            wait_send(k, s, b_send)


def finish(slots, own_w, got_w, own_d, got_d, lo, dt, dg, gate, up, down, lo_out, dt_out, dg_out):
    lo_out[...] = lo[...]
    dt_out[...] = dt[...]
    dg_out[...] = dg[...]
    last = pl.program_id(0) == slots - 1
    jobs = (
        (own_w.at[0, 0], got_w.at[0, 0, 0], got_w.at[0, 1, 0], gate.at[0]),
        (own_w.at[1, 0], got_w.at[1, 0, 0], got_w.at[1, 1, 0], up.at[0]),
        (own_d.at[0], got_d.at[0, 0], got_d.at[1, 0], down.at[0]),
    )

    @pl.when(last)
    def _():
        for own, one, two, out in jobs:
            both = one[...].astype(F32) + two[...].astype(F32)
            out[...] = (own[...].astype(F32) + both).astype(BF16)

    @pl.when(jnp.logical_not(last))
    def _():
        for own, _, _, out in jobs:
            out[...] = own[...]


def on_device(n, ring, tokens, expert_ids, gate_weights, slot_of_expert, w_gate, w_up, w_down, d_out):
    slots, width, ff = w_gate.shape
    tok_rows, tops = expert_ids.shape
    experts = slots * n
    capacity = tok_rows * tops * 7 // (4 * experts)
    pad = -(-capacity // 16) * 16
    rows = n * pad
    chunk = width // ring

    wide = jnp.arange(experts, dtype=jnp.int32)
    slot = jnp.sum(jnp.where(expert_ids[:, :, None] == wide, slot_of_expert, 0), axis=2)
    named = slot[:, :, None] == wide
    earlier = jnp.arange(tok_rows)[:, None] > jnp.arange(tok_rows)[None, :]
    before = jnp.dot(
        earlier.astype(BF16), jnp.any(named, axis=1).astype(BF16), preferred_element_type=F32
    )
    rank = jnp.sum(jnp.where(named, before[:, None, :], 0.0), axis=2).astype(jnp.int32)
    pos = (slot % slots) * rows + (slot // slots) * pad + rank

    vmem = pl.BlockSpec(memory_space=pltpu.VMEM)
    hbm = pl.BlockSpec(memory_space=pl.ANY)
    gates_pos = jnp.concatenate([gate_weights.T, pos.T.astype(F32)], axis=0)
    out = pl.pallas_call(
        functools.partial(kernel, n, ring),
        out_shape=[
            jax.ShapeDtypeStruct((tok_rows, width), BF16),
            jax.ShapeDtypeStruct((tok_rows, width), BF16),
            jax.ShapeDtypeStruct((tops, tok_rows), F32),
            jax.ShapeDtypeStruct((2, slots, chunk, ff), BF16),
            jax.ShapeDtypeStruct((slots, ff, chunk), BF16),
            jax.ShapeDtypeStruct((2, slots, n, pad, width), BF16),
            jax.ShapeDtypeStruct((2, 2, slots, chunk, ff), BF16),
            jax.ShapeDtypeStruct((2, slots, ff, chunk), BF16),
        ],
        in_specs=[vmem] * 3 + [hbm] * 3,
        out_specs=[vmem] * 3 + [hbm] * 5,
        scratch_shapes=[
            pltpu.VMEM((2, slots, n, pad, width), BF16),
            pltpu.VMEM((2, slots, n, pad, width), BF16),
            pltpu.VMEM((width, ff), BF16),
            pltpu.VMEM((width, ff), BF16),
            pltpu.VMEM((ff, width), BF16),
            pltpu.VMEM((2, rows, ff), F32),
            pltpu.VMEM((3, rows, ff), BF16),
            pltpu.VMEM((2, slots, ring, chunk, ff), BF16),
            pltpu.VMEM((slots, ring, ff, chunk), BF16),
            pltpu.VMEM((2, slots, 2, chunk // 2, ff), BF16),
            pltpu.VMEM((slots, 2, ff // 2, chunk), BF16),
            pltpu.VMEM((2, chunk, ff), BF16),
            pltpu.VMEM((2, ff, chunk), BF16),
            pltpu.SemaphoreType.DMA((2, slots)),
            pltpu.SemaphoreType.DMA((2, slots)),
            pltpu.SemaphoreType.DMA((2, slots)),
            pltpu.SemaphoreType.DMA((2, slots)),
            pltpu.SemaphoreType.DMA((3,)),
            pltpu.SemaphoreType.DMA((slots, 3, 3, 2)),
            pltpu.SemaphoreType.DMA((slots, 3, 3, 2)),
            pltpu.SemaphoreType.DMA((2, slots)),
            pltpu.SemaphoreType.DMA((slots, 3)),
            pltpu.SemaphoreType.DMA((2,)),
        ],
        compiler_params=pltpu.CompilerParams(
            collective_id=0, has_side_effects=True, vmem_limit_bytes=63 * 1024 * 1024
        ),
    )(gates_pos, tokens, d_out, w_gate, w_up, w_down)
    layer_out, d_tokens, d_gates, own_w, own_d, _, got_w, got_d = out

    parts = 4
    w_rows, d_rows, t_rows = chunk // parts, ff // parts, tok_rows // (parts * slots)

    def late(s, j):
        return jnp.where(s == slots - 1, j, 0)

    w_out = pl.BlockSpec((1, w_rows, ff), lambda s, j: (s, j, 0))
    d_out_spec = pl.BlockSpec((1, d_rows, chunk), lambda s, j: (s, j, 0))
    t_spec = pl.BlockSpec((t_rows, width), lambda s, j: (s * parts + j, 0))
    g_spec = pl.BlockSpec((tops, tok_rows), lambda s, j: (0, 0))
    grad_gate, grad_up, grad_down, layer_out, d_tokens, d_gates = pl.pallas_call(
        functools.partial(finish, slots),
        grid=(slots, parts),
        out_shape=[
            jax.ShapeDtypeStruct((slots, chunk, ff), BF16),
            jax.ShapeDtypeStruct((slots, chunk, ff), BF16),
            jax.ShapeDtypeStruct((slots, ff, chunk), BF16),
            jax.ShapeDtypeStruct((tok_rows, width), BF16),
            jax.ShapeDtypeStruct((tok_rows, width), BF16),
            jax.ShapeDtypeStruct((tops, tok_rows), F32),
        ],
        in_specs=[
            pl.BlockSpec((2, 1, w_rows, ff), lambda s, j: (0, s, j, 0)),
            pl.BlockSpec((2, 2, 1, w_rows, ff), lambda s, j: (0, 0, slots - 1, late(s, j), 0)),
            d_out_spec,
            pl.BlockSpec((2, 1, d_rows, chunk), lambda s, j: (0, slots - 1, late(s, j), 0)),
            t_spec, t_spec, g_spec,
        ],
        out_specs=[w_out, w_out, d_out_spec, t_spec, t_spec, g_spec],
        compiler_params=pltpu.CompilerParams(vmem_limit_bytes=63 * 1024 * 1024),
    )(own_w, got_w, own_d, got_d, layer_out, d_tokens, d_gates)
    return layer_out, d_tokens, d_gates.T, grad_gate, grad_up, grad_down


def solution(mesh):
    token = P(("dp", "expert"), None)
    weight = P("expert", None, None)
    return jax.shard_map(
        functools.partial(on_device, mesh.shape["expert"], mesh.shape["dp"]),
        mesh=mesh,
        in_specs=(token, token, token, P(), weight, weight, weight, token),
        out_specs=(
            token, token, token,
            P("expert", "dp", None), P("expert", "dp", None), P("expert", None, "dp"),
        ),
        check_vma=False,
    )
```

```python
import functools

import jax
import jax.numpy as jnp
from jax import lax
from jax.experimental import pallas as pl
from jax.experimental.pallas import tpu as pltpu
from jax.sharding import PartitionSpec as P

MESH = pl.DeviceIdType.MESH
STRIDE = 3
FORWARD_AT = (1, 1, 1, 1)
RETURN_AT = (1, 1, 2, 3)
LAST_AT = (0, 0, 0, 0)
F32 = jnp.float32
BF16 = jnp.bfloat16
NT = (((1,), (1,)), ((), ()))
TN = (((0,), (0,)), ((), ()))


def mm(a, b):
    return jnp.dot(a, b, preferred_element_type=F32)


def mm_nt(a, b):
    return lax.dot_general(a, b, NT, preferred_element_type=F32)


def mm_tn(a, b):
    return lax.dot_general(a, b, TN, preferred_element_type=F32)


def kernel(
    n, ring, gates_pos, tok, dout, wg_h, wu_h, wd_h,
    lo, dt, dg, own_w, own_d, ret, r2w, r2d,
    send, land, wg, wu, wd, act, hid, pw, pd, r1w, r1d, tw, td,
    f_send, f_recv, b_send, b_recv, w_sem, g_send, g_recv, l_sem, o_sem, t_sem,
):
    me = lax.axis_index("expert")
    r = lax.axis_index("dp")
    right, left, opp = lax.rem(r + 1, ring), lax.rem(r + 3, ring), lax.rem(r + 2, ring)
    slots, _, pad, width = send.shape[1:]
    rows = n * pad
    ff = wg.shape[1]
    chunk = width // ring
    ft = 256
    tops = gates_pos.shape[0] // 2
    tok_rows = tok.shape[0]

    barrier = pltpu.get_barrier_semaphore()

    def greet(i, _):
        pl.semaphore_signal(
            barrier, inc=1, device_id={"expert": lax.rem(me + i, n)}, device_id_type=MESH
        )
        return 0

    lax.fori_loop(1, n, greet, 0)
    for side in (right, left):
        pl.semaphore_signal(barrier, inc=1, device_id={"dp": side}, device_id_type=MESH)

    def weight_copies(s):
        return [
            pltpu.make_async_copy(src.at[s], dst, w_sem.at[j])
            for j, (src, dst) in enumerate(((wg_h, wg), (wu_h, wu), (wd_h, wd)))
        ]

    for copy in weight_copies(0):
        copy.start()

    def fill(s):
        spot = lax.broadcasted_iota(jnp.int32, (rows, tok_rows), 0) + s * rows
        picked = jnp.zeros(spot.shape, F32)
        weight = jnp.zeros(spot.shape, F32)
        for k in range(tops):
            hit = gates_pos[tops + k : tops + k + 1, :].astype(jnp.int32) == spot
            picked = jnp.where(hit, 1.0, picked)
            weight = jnp.where(hit, gates_pos[k : k + 1, :], weight)
        picked = picked.astype(BF16)
        weight = jnp.sum(weight, axis=1, keepdims=True)

        def tile(j, _):
            cols = pl.ds(pl.multiple_of(j * chunk, chunk), chunk)
            send[0, s, :, :, cols] = mm(picked, tok[:, cols]).astype(BF16).reshape(n, pad, chunk)
            rows_d = mm(picked, dout[:, cols]) * weight
            send[1, s, :, :, cols] = rows_d.astype(BF16).reshape(n, pad, chunk)
            return 0

        lax.fori_loop(0, width // chunk, tile, 0)

    def keep(k, s, dst, r_sem):
        pltpu.make_async_copy(send.at[k, s, me], dst.at[k, s, me], r_sem.at[k, s]).start()

    def row_copy(k, s, peer, dst, s_sem, r_sem):
        return pltpu.make_async_remote_copy(
            src_ref=send.at[k, s, peer],
            dst_ref=dst.at[k, s, me],
            send_sem=s_sem.at[k, s],
            recv_sem=r_sem.at[k, s],
            device_id={"expert": peer},
            device_id_type=MESH,
        )

    def send_part(k, s, core, dst, s_sem, r_sem):
        def go(i, _):
            chip = lax.rem(me // 2 + STRIDE * i, n // 2)
            peer = chip * 2 + core

            @pl.when(peer != me)
            def _():
                row_copy(k, s, peer, dst, s_sem, r_sem).start()

            return 0

        if core == 0:
            keep(k, s, dst, r_sem)
        lax.fori_loop(0, n // 2, go, 0)

    def forward_part(q, s):
        send_part(q % 2, s, q // 2, land, f_send, f_recv)

    def return_part(q, s):
        send_part(q // 2, s, q % 2, ret, b_send, b_recv)

    def next_parts(point, s):
        @pl.when(s + 1 < slots)
        def _():
            for q in range(4):
                if FORWARD_AT[q] == point:
                    forward_part(q, s + 1)

        @pl.when(s > 0)
        def _():
            for q in range(4):
                if RETURN_AT[q] == point:
                    return_part(q, s - 1)

    def wait_recv(k, s, dst, r_sem):
        pltpu.make_async_copy(dst.at[k, s], dst.at[k, s], r_sem.at[k, s]).wait()

    def wait_send(k, s, s_sem):
        part = send.at[k, s, pl.ds(0, n - 1)]
        pltpu.make_async_copy(part, part, s_sem.at[k, s]).wait()

    items = (
        (pd, r1d, r2d, own_d, td),
        (pw.at[0], r1w.at[0], r2w.at[0], own_w.at[0], tw),
        (pw.at[1], r1w.at[1], r2w.at[1], own_w.at[1], tw),
    )

    def ring_copy(item, s, step, side):
        part, first, second, _, _ = items[item]
        half = part.shape[2] // 2
        low, high = pl.ds(0, half), pl.ds(half, half)
        near = right if side == 0 else left
        if step == 0:
            rows_s = low if side == 0 else high
            src, dst = part.at[s, opp, rows_s], first.at[s, side]
        else:
            rows_s = (high if side == 0 else low) if step == 1 else (low if side == 0 else high)
            src, dst = part.at[s, near, rows_s], second.at[side, s, rows_s]
        return pltpu.make_async_remote_copy(
            src_ref=src,
            dst_ref=dst,
            send_sem=g_send.at[s, item, step, side],
            recv_sem=g_recv.at[s, item, step, side],
            device_id={"dp": near},
            device_id_type=MESH,
        )

    def ring_start(item, s):
        for step in (0, 1):
            for side in (0, 1):
                ring_copy(item, s, step, side).start()

    def add_rows(dst, src, count):
        block = 64

        def go(j, _):
            at = pl.ds(pl.multiple_of(j * block, block), block)
            dst[at, :] = (dst[at, :].astype(F32) + src[at, :].astype(F32)).astype(BF16)
            return 0

        lax.fori_loop(0, count // block, go, 0)

    def ring_middle(item, s):
        part, first, _, _, _ = items[item]
        half = part.shape[2] // 2
        for side in (0, 1):
            near = right if side == 0 else left
            at = pl.ds(0, half) if side == 0 else pl.ds(half, half)
            ring_copy(item, s, 0, side).wait_recv()
            add_rows(part.at[s, near, at], first.at[s, side], half)
            ring_copy(item, s, 2, side).start()

    def own_copy(item, s):
        part, _, _, own, _ = items[item]
        return pltpu.make_async_copy(part.at[s, r], own.at[s], o_sem.at[s, item])

    def ring_end(item, s):
        part, _, second, _, temp = items[item]
        loads = [
            pltpu.make_async_copy(second.at[side, s], temp.at[side], t_sem.at[side])
            for side in (0, 1)
        ]
        for side in (0, 1):
            for step in (1, 2):
                ring_copy(item, s, step, side).wait_recv()
            loads[side].start()
        for copy in loads:
            copy.wait()
        block = 64
        total = part.at[s, r]

        def go(j, _):
            at = pl.ds(pl.multiple_of(j * block, block), block)
            both = temp[0, at, :].astype(F32) + temp[1, at, :].astype(F32)
            total[at, :] = (total[at, :].astype(F32) + both).astype(BF16)
            return 0

        lax.fori_loop(0, part.shape[2] // block, go, 0)
        own_copy(item, s).start()

    def rows_of(k, s, cols):
        return land[k, s, :, :, cols].reshape(rows, -1)

    def compute(s, _):
        for copy in weight_copies(s):
            copy.wait()
        wait_recv(0, s, land, f_recv)

        def first(j, _):
            cols = pl.ds(pl.multiple_of(j * ft, ft), ft)
            x = rows_of(0, s, slice(None))
            gate = mm(x, wg[:, cols])
            up = mm(x, wu[:, cols])
            sigma = jax.nn.sigmoid(gate)
            silu = gate * sigma
            hid[0, :, cols] = (silu * up).astype(BF16)
            act[0, :, cols] = up * sigma * (1.0 + gate * (1.0 - sigma))
            act[1, :, cols] = silu
            return 0

        lax.fori_loop(0, ff // ft, first, 0)
        wait_send(0, s, f_send)

        def out_tile(j, _):
            cols = pl.ds(pl.multiple_of(j * chunk, chunk), chunk)
            send[0, s, :, :, cols] = mm(hid[0], wd[:, cols]).astype(BF16).reshape(n, pad, chunk)
            return 0

        lax.fori_loop(0, ring, out_tile, 0)
        next_parts(0, s)
        wait_recv(1, s, land, f_recv)

        def down_tile(j, _):
            at = lax.rem(opp + j, ring)
            cols = pl.ds(pl.multiple_of(at * chunk, chunk), chunk)
            pd[s, at] = mm_tn(hid[0], rows_of(1, s, cols)).astype(BF16)

            @pl.when(j == 0)
            def _():
                for side in (0, 1):
                    ring_copy(0, s, 0, side).start()

            return 0

        lax.fori_loop(0, ring, down_tile, 0)
        for side in (0, 1):
            ring_copy(0, s, 1, side).start()
        @pl.when(s == slots - 1)
        def _():
            own_copy(0, s).start()

        next_parts(1, s)

        def back(j, _):
            cols = pl.ds(pl.multiple_of(j * ft, ft), ft)
            d_hid = mm_nt(rows_of(1, s, slice(None)), wd[cols, :])
            hid[1, :, cols] = (d_hid * act[0, :, cols]).astype(BF16)
            hid[2, :, cols] = (d_hid * act[1, :, cols]).astype(BF16)
            return 0

        lax.fori_loop(0, ff // ft, back, 0)
        for item in (0, 1):

            def up_tile(j, _):
                cols = pl.ds(pl.multiple_of(j * chunk, chunk), chunk)
                pw[item, s, j] = mm_tn(rows_of(0, s, cols), hid[1 + item]).astype(BF16)
                return 0

            lax.fori_loop(0, ring, up_tile, 0)
            ring_start(1 + item, s)

            @pl.when(s == slots - 1)
            def _():
                own_copy(1 + item, s).start()

            next_parts(2 + item, s)
        wait_send(1, s, f_send)

        def in_tile(j, _):
            cols = pl.ds(pl.multiple_of(j * chunk, chunk), chunk)
            total = mm_nt(hid[1], wg[cols, :]) + mm_nt(hid[2], wu[cols, :])
            send[1, s, :, :, cols] = total.astype(BF16).reshape(n, pad, chunk)
            return 0

        lax.fori_loop(0, ring, in_tile, 0)
        @pl.when(s + 1 < slots)
        def _():
            for copy in weight_copies(s + 1):
                copy.start()

        for q in range(4):

            @pl.when(s == slots - 1)
            def _():
                for part in range(4):
                    if LAST_AT[part] == q:
                        return_part(part, s)

            if q < 3:
                ring_middle(q, s)
        return 0

    fill(0)
    pl.semaphore_wait(barrier, n + 1)
    for q in range(4):
        forward_part(q, 0)
    for s in range(1, slots):
        fill(s)
    lax.fori_loop(0, slots, compute, 0)

    spots = slots * rows
    spot = lax.broadcasted_iota(jnp.int32, (tok_rows, spots), 1)
    columns = gates_pos[...].T
    hits = [columns[:, tops + k : tops + k + 1].astype(jnp.int32) == spot for k in range(tops)]
    hits = [jnp.where(hit, 1.0, 0.0) for hit in hits]
    whole = sum(hits).astype(BF16)
    hits = [hit.astype(BF16) for hit in hits]

    def fetch(k):
        loads = [
            pltpu.make_async_copy(ret.at[k, s], land.at[k, s], l_sem.at[k, s]) for s in range(slots)
        ]
        for s in range(slots):
            wait_recv(k, s, ret, b_recv)
            loads[s].start()
        for s in range(slots):
            loads[s].wait()

    for s in range(slots - 1):
        for item in range(3):
            ring_end(item, s)
    fetch(0)

    def combine(j, sums):
        cols = pl.ds(pl.multiple_of(j * chunk, chunk), chunk)
        outs = land[0, :, :, :, cols].reshape(spots, chunk)
        d_here = dout[:, cols].astype(F32)
        layer = jnp.zeros(d_here.shape, F32)
        result = []
        for k in range(tops):
            got = mm(hits[k], outs)
            layer = layer + columns[:, k : k + 1] * got
            result.append(sums[k] + jnp.sum(d_here * got, axis=1, keepdims=True))
        lo[:, cols] = layer.astype(BF16)
        return tuple(result)

    zero = jnp.zeros((tok_rows, 1), F32)
    sums = lax.fori_loop(0, ring, combine, (zero,) * tops)
    lane = lax.broadcasted_iota(jnp.int32, (tok_rows, 128), 1)
    table = jnp.zeros(lane.shape, F32)
    for k in range(tops):
        table = jnp.where(lane == k, sums[k], table)
    dg[...] = table.T[:tops]

    fetch(1)

    def combine_in(j, _):
        cols = pl.ds(pl.multiple_of(j * chunk, chunk), chunk)
        dt[:, cols] = mm(whole, land[1, :, :, :, cols].reshape(spots, chunk)).astype(BF16)
        return 0

    lax.fori_loop(0, ring, combine_in, 0)

    for s in range(slots):
        for item in range(3):
            own_copy(item, s).wait()
            for side in (0, 1):
                if s == slots - 1:
                    for step in (1, 2):
                        ring_copy(item, s, step, side).wait_recv()
                for step in range(3):
                    ring_copy(item, s, step, side).wait_send()
        for k in (0, 1):
            wait_send(k, s, b_send)


def finish(slots, own_w, got_w, own_d, got_d, lo, dt, dg, gate, up, down, lo_out, dt_out, dg_out):
    lo_out[...] = lo[...]
    dt_out[...] = dt[...]
    dg_out[...] = dg[...]
    last = pl.program_id(0) == slots - 1
    jobs = (
        (own_w.at[0, 0], got_w.at[0, 0, 0], got_w.at[0, 1, 0], gate.at[0]),
        (own_w.at[1, 0], got_w.at[1, 0, 0], got_w.at[1, 1, 0], up.at[0]),
        (own_d.at[0], got_d.at[0, 0], got_d.at[1, 0], down.at[0]),
    )

    @pl.when(last)
    def _():
        for own, one, two, out in jobs:
            both = one[...].astype(F32) + two[...].astype(F32)
            out[...] = (own[...].astype(F32) + both).astype(BF16)

    @pl.when(jnp.logical_not(last))
    def _():
        for own, _, _, out in jobs:
            out[...] = own[...]


def on_device(n, ring, tokens, expert_ids, gate_weights, slot_of_expert, w_gate, w_up, w_down, d_out):
    slots, width, ff = w_gate.shape
    tok_rows, tops = expert_ids.shape
    experts = slots * n
    capacity = tok_rows * tops * 7 // (4 * experts)
    pad = -(-capacity // 16) * 16
    rows = n * pad
    chunk = width // ring

    wide = jnp.arange(experts, dtype=jnp.int32)
    slot = jnp.sum(jnp.where(expert_ids[:, :, None] == wide, slot_of_expert, 0), axis=2)
    named = slot[:, :, None] == wide
    earlier = jnp.arange(tok_rows)[:, None] > jnp.arange(tok_rows)[None, :]
    before = jnp.dot(
        earlier.astype(BF16), jnp.any(named, axis=1).astype(BF16), preferred_element_type=F32
    )
    rank = jnp.sum(jnp.where(named, before[:, None, :], 0.0), axis=2).astype(jnp.int32)
    pos = (slot % slots) * rows + (slot // slots) * pad + rank

    vmem = pl.BlockSpec(memory_space=pltpu.VMEM)
    hbm = pl.BlockSpec(memory_space=pl.ANY)
    gates_pos = jnp.concatenate([gate_weights.T, pos.T.astype(F32)], axis=0)
    out = pl.pallas_call(
        functools.partial(kernel, n, ring),
        out_shape=[
            jax.ShapeDtypeStruct((tok_rows, width), BF16),
            jax.ShapeDtypeStruct((tok_rows, width), BF16),
            jax.ShapeDtypeStruct((tops, tok_rows), F32),
            jax.ShapeDtypeStruct((2, slots, chunk, ff), BF16),
            jax.ShapeDtypeStruct((slots, ff, chunk), BF16),
            jax.ShapeDtypeStruct((2, slots, n, pad, width), BF16),
            jax.ShapeDtypeStruct((2, 2, slots, chunk, ff), BF16),
            jax.ShapeDtypeStruct((2, slots, ff, chunk), BF16),
        ],
        in_specs=[vmem] * 3 + [hbm] * 3,
        out_specs=[vmem] * 3 + [hbm] * 5,
        scratch_shapes=[
            pltpu.VMEM((2, slots, n, pad, width), BF16),
            pltpu.VMEM((2, slots, n, pad, width), BF16),
            pltpu.VMEM((width, ff), BF16),
            pltpu.VMEM((width, ff), BF16),
            pltpu.VMEM((ff, width), BF16),
            pltpu.VMEM((2, rows, ff), F32),
            pltpu.VMEM((3, rows, ff), BF16),
            pltpu.VMEM((2, slots, ring, chunk, ff), BF16),
            pltpu.VMEM((slots, ring, ff, chunk), BF16),
            pltpu.VMEM((2, slots, 2, chunk // 2, ff), BF16),
            pltpu.VMEM((slots, 2, ff // 2, chunk), BF16),
            pltpu.VMEM((2, chunk, ff), BF16),
            pltpu.VMEM((2, ff, chunk), BF16),
            pltpu.SemaphoreType.DMA((2, slots)),
            pltpu.SemaphoreType.DMA((2, slots)),
            pltpu.SemaphoreType.DMA((2, slots)),
            pltpu.SemaphoreType.DMA((2, slots)),
            pltpu.SemaphoreType.DMA((3,)),
            pltpu.SemaphoreType.DMA((slots, 3, 3, 2)),
            pltpu.SemaphoreType.DMA((slots, 3, 3, 2)),
            pltpu.SemaphoreType.DMA((2, slots)),
            pltpu.SemaphoreType.DMA((slots, 3)),
            pltpu.SemaphoreType.DMA((2,)),
        ],
        compiler_params=pltpu.CompilerParams(
            collective_id=0, has_side_effects=True, vmem_limit_bytes=63 * 1024 * 1024
        ),
    )(gates_pos, tokens, d_out, w_gate, w_up, w_down)
    layer_out, d_tokens, d_gates, own_w, own_d, _, got_w, got_d = out

    parts = 2
    w_rows, d_rows, t_rows = chunk // parts, ff // parts, tok_rows // (parts * slots)

    def late(s, j):
        return jnp.where(s == slots - 1, j, 0)

    w_out = pl.BlockSpec((1, w_rows, ff), lambda s, j: (s, j, 0))
    d_out_spec = pl.BlockSpec((1, d_rows, chunk), lambda s, j: (s, j, 0))
    t_spec = pl.BlockSpec((t_rows, width), lambda s, j: (s * parts + j, 0))
    g_spec = pl.BlockSpec((tops, tok_rows), lambda s, j: (0, 0))
    grad_gate, grad_up, grad_down, layer_out, d_tokens, d_gates = pl.pallas_call(
        functools.partial(finish, slots),
        grid=(slots, parts),
        out_shape=[
            jax.ShapeDtypeStruct((slots, chunk, ff), BF16),
            jax.ShapeDtypeStruct((slots, chunk, ff), BF16),
            jax.ShapeDtypeStruct((slots, ff, chunk), BF16),
            jax.ShapeDtypeStruct((tok_rows, width), BF16),
            jax.ShapeDtypeStruct((tok_rows, width), BF16),
            jax.ShapeDtypeStruct((tops, tok_rows), F32),
        ],
        in_specs=[
            pl.BlockSpec((2, 1, w_rows, ff), lambda s, j: (0, s, j, 0)),
            pl.BlockSpec((2, 2, 1, w_rows, ff), lambda s, j: (0, 0, slots - 1, late(s, j), 0)),
            d_out_spec,
            pl.BlockSpec((2, 1, d_rows, chunk), lambda s, j: (0, slots - 1, late(s, j), 0)),
            t_spec, t_spec, g_spec,
        ],
        out_specs=[w_out, w_out, d_out_spec, t_spec, t_spec, g_spec],
        compiler_params=pltpu.CompilerParams(vmem_limit_bytes=63 * 1024 * 1024),
    )(own_w, got_w, own_d, got_d, layer_out, d_tokens, d_gates)
    return layer_out, d_tokens, d_gates.T, grad_gate, grad_up, grad_down


def solution(mesh):
    token = P(("dp", "expert"), None)
    weight = P("expert", None, None)
    return jax.shard_map(
        functools.partial(on_device, mesh.shape["expert"], mesh.shape["dp"]),
        mesh=mesh,
        in_specs=(token, token, token, P(), weight, weight, weight, token),
        out_specs=(
            token, token, token,
            P("expert", "dp", None), P("expert", "dp", None), P("expert", None, "dp"),
        ),
        check_vma=False,
    )
```
